256 devices in a mesh: lat: 64 (over y_lo, x, z), lev: 4 (over y_hi, core).
Axes of the slice: x: 4, y: 4 (y_hi: 2, y_lo: 2; y = y_hi * 2 + y_lo), z: 8, core: 2. Of those that a mesh axis runs over, the one named last changes fastest.
Arguments:
- zonal_velocity: float32 [16, 256, 2880], P('lev', 'lat'), may hold values from -1 to 1
- meridional_velocity: float32 [16, 256, 2880], P('lev', 'lat'), may hold values from -1 to 1
- heat_anomaly: float32 [16, 256, 2880], P('lev', 'lat'), may hold values from -6 to 6
- layer_pressure_depth: float32 [16, 256, 2880], P('lev', 'lat'), may hold values from 0.8 to 1.2
- reference_layer_shares: float32 [16], replicated, may hold values from 0.5 to 2
Outputs:
- temp_remapped: float32 [16, 256, 2880], P(None, 'lat', 'lev')
- u_remapped: float32 [16, 256, 2880], P(None, 'lat', 'lev')
- v_remapped: float32 [16, 256, 2880], P(None, 'lat', 'lev')
- thick_remapped: float32 [16, 256, 2880], P(None, 'lat', 'lev')
The draws below stay inside these ranges and needn't reach their ends.
All inputs are finite; a program needn't handle non-finite values.
Results may differ from the reference program's by a relative error of at most 0.0003.
Values sent between devices are 32-bit elements; how exact they have to be, the bound alone decides.
A program may use at most 192 MiB of HBM per device.

```python
import math
import jax
import jax.numpy as jnp
from jax import lax

MERIDIAN_NUMBER = 2880
PARALLEL_BANDS = 256
LAYER_NUMBER = 16


def block_scale(rng, dims, cuts, smallest, top_value):
    def one(position, parts):
        heights = jax.random.uniform(jax.random.fold_in(jax.random.fold_in(rng, 6), position), (parts,), jnp.float32, smallest / len(cuts), top_value / len(cuts))
        return jnp.repeat(jnp.exp(heights), dims[position] // parts).reshape((-1,) + (1,) * (len(dims) - position - 1))

    loudness = one(*cuts[0])
    for cut in cuts[1:]:
        loudness = loudness * one(*cut)
    return loudness


def gaussian(stream_key, shape, deviation, bound, shards=(), kind=jnp.bfloat16):
    entries = deviation * jax.random.normal(stream_key, shape, jnp.float32)
    if shards:
        entries = entries * block_scale(stream_key, shape, shards, -0.22, 0.18)
    return jnp.clip(entries, -bound, bound).astype(kind)


def setup_inputs(seed: int = 0) -> dict:
    arg_keys = jax.random.split(jax.random.key(seed), 6)
    return {
        "zonal_velocity": jnp.clip(jax.random.uniform(arg_keys[0], (LAYER_NUMBER, PARALLEL_BANDS, MERIDIAN_NUMBER), jnp.float32, -1.0, 1.0) * block_scale(arg_keys[0], (LAYER_NUMBER, PARALLEL_BANDS, MERIDIAN_NUMBER), ((0, 4), (1, 64)), -0.4, 0.0), -1.0, 1.0),
        "meridional_velocity": jnp.clip(jax.random.uniform(arg_keys[1], (LAYER_NUMBER, PARALLEL_BANDS, MERIDIAN_NUMBER), jnp.float32, -1.0, 1.0) * block_scale(arg_keys[1], (LAYER_NUMBER, PARALLEL_BANDS, MERIDIAN_NUMBER), ((0, 4), (1, 64)), -0.4, 0.0), -1.0, 1.0),
        "heat_anomaly": gaussian(arg_keys[2], (LAYER_NUMBER, PARALLEL_BANDS, MERIDIAN_NUMBER), 1.0, 6.0, ((0, 4), (1, 64)), jnp.float32),
        "layer_pressure_depth": jnp.clip(0.8 + 0.40000004 * jax.random.uniform(arg_keys[3], (LAYER_NUMBER, PARALLEL_BANDS, MERIDIAN_NUMBER), jnp.float32) ** block_scale(arg_keys[3], (LAYER_NUMBER, PARALLEL_BANDS, MERIDIAN_NUMBER), ((0, 4), (1, 64)), -0.2, 0.2), 0.8, 1.2),
        "reference_layer_shares": jnp.clip(jnp.exp(jax.random.uniform(arg_keys[4], (LAYER_NUMBER,), jnp.float32, math.log(0.5), math.log(2.0))), 0.5, 2.0),
    }


SPEED = 0.04
QUARTER = math.cos(math.pi / 4.0)
SPACING = 180.0 / 1440.0


def minmod(left_diff, right_diff):
    return 0.5 * (jnp.sign(left_diff) + jnp.sign(right_diff)) * jnp.minimum(jnp.abs(left_diff), jnp.abs(right_diff))


def upwind_face(lower_cell, upper_cell, lower_slope, upper_slope, courant):
    return jnp.where(courant >= 0.0, lower_cell + 0.5 * (1.0 - courant) * lower_slope, upper_cell - 0.5 * (1.0 + courant) * upper_slope)


def zonal_change(quants, zonal_wind):
    courant = SPEED * (zonal_wind + jnp.roll(zonal_wind, -1, axis=-1))
    slopes = minmod(quants - jnp.roll(quants, 1, axis=-1), jnp.roll(quants, -1, axis=-1) - quants)
    face_value = upwind_face(quants, jnp.roll(quants, -1, axis=-1), slopes, jnp.roll(slopes, -1, axis=-1), courant)
    face_flux = courant * face_value
    return face_flux - jnp.roll(face_flux, 1, axis=-1)


def meridional_change(lower_cell, upper_cell, lower_slope, upper_slope, lower_wind, upper_wind, cos_face, cos_center):
    courant = SPEED * (lower_wind + upper_wind)
    face_flux = courant * cos_face[:, None] * upwind_face(lower_cell, upper_cell, lower_slope, upper_slope, courant)
    return (face_flux[..., 1:, :] - face_flux[..., :-1, :]) / cos_center[:, None]


def center_cos(row_index):
    angle = ((row_index.astype(jnp.float32) + 0.5) * SPACING - 90.0) * (math.pi / 180.0)
    return jnp.cos(angle)


def face_cos(face_index):
    angle = (face_index.astype(jnp.float32) * SPACING - 90.0) * (math.pi / 180.0)
    return jnp.where(face_index == 0, 0.0, jnp.cos(angle))


def polar_filter(fields, cos_ratio):
    lon_count = fields.shape[-1]
    wave_number = jnp.arange(lon_count // 2 + 1).astype(jnp.float32)
    sine_wave = jnp.sin(wave_number * (math.pi / lon_count))
    damping = (cos_ratio[:, None] / jnp.maximum(sine_wave[None, :], cos_ratio[:, None])) ** 2
    spectrum = jnp.fft.rfft(fields, axis=-1) * damping
    return jnp.fft.irfft(spectrum, n=lon_count, axis=-1)


def remap_column(fields, thick, shares):
    upper_src = jnp.cumsum(thick, axis=0)
    lower_src = upper_src - thick
    column_total = upper_src[-1]
    target = column_total[None, :] * shares[:, None]
    upper_dst = column_total[None, :] * jnp.cumsum(shares)[:, None]
    lower_dst = upper_dst - target
    intersection = jnp.maximum(0.0, jnp.minimum(upper_dst[:, None], upper_src[None]) - jnp.maximum(lower_dst[:, None], lower_src[None]))
    remapped = [jnp.sum(intersection * fields[field_index][None], axis=1) / target for field_index in range(3)]
    return jnp.stack(remapped + [target])


def reference(zonal_velocity, meridional_velocity, heat_anomaly, layer_pressure_depth, reference_layer_shares):
    row_index = jnp.arange(PARALLEL_BANDS)
    face_index = jnp.arange(PARALLEL_BANDS + 1)
    cos_center = center_cos(row_index)
    cos_face = face_cos(face_index)
    cos_ratio = cos_center / QUARTER

    def one_layer_slice(level_args):
        zonal_wind, merid_wind, temp_level, thick_level = level_args
        quants = jnp.stack([thick_level, thick_level * temp_level, thick_level * zonal_wind, thick_level * merid_wind])
        padded = jnp.pad(quants, ((0, 0), (2, 2), (0, 0)))
        wind_pad = jnp.pad(merid_wind, ((2, 2), (0, 0)))
        slopes = minmod(padded[:, 1:-1] - padded[:, :-2], padded[:, 2:] - padded[:, 1:-1])
        change_y = meridional_change(padded[:, 1:-2], padded[:, 2:-1], slopes[:, :-1], slopes[:, 1:], wind_pad[1:-2], wind_pad[2:-1], cos_face, cos_center)
        updated = quants - zonal_change(quants, zonal_wind) - change_y
        fields = updated[1:] / updated[0]
        smoothed = polar_filter(fields, cos_ratio)
        return jnp.concatenate([smoothed, updated[:1]], axis=0)

    layered_arrays = lax.map(one_layer_slice, (zonal_velocity, meridional_velocity, heat_anomaly, layer_pressure_depth))
    shares = reference_layer_shares / jnp.sum(reference_layer_shares)
    columns = jnp.transpose(layered_arrays, (2, 1, 0, 3))
    remapped = lax.map(lambda column_set: remap_column(column_set[:3], column_set[3], shares), columns)
    result = jnp.transpose(remapped, (1, 2, 0, 3))
    return result[0], result[1], result[2], result[3]
```

```python
import math

import jax
import jax.numpy as jnp
from jax import lax
from jax.sharding import PartitionSpec as P

SPEED = 0.04
QUARTER = math.cos(math.pi / 4.0)
SPACING = 180.0 / 1440.0


def extended(block, sides, width):
    for axis, dim in sides:
        count = lax.axis_size(axis)
        forward = [(i, i + 1) for i in range(count - 1)]
        backward = [(target, source) for source, target in forward]
        low = lax.ppermute(
            lax.slice_in_dim(block, block.shape[dim] - width, None, axis=dim), axis, forward
        )
        high = lax.ppermute(lax.slice_in_dim(block, 0, width, axis=dim), axis, backward)
        block = jnp.concatenate([low, block, high], axis=dim)
    return block


def minmod(left_diff, right_diff):
    return (
        0.5
        * (jnp.sign(left_diff) + jnp.sign(right_diff))
        * jnp.minimum(jnp.abs(left_diff), jnp.abs(right_diff))
    )


def upwind_face(lower_cell, upper_cell, lower_slope, upper_slope, courant):
    return jnp.where(
        courant >= 0.0,
        lower_cell + 0.5 * (1.0 - courant) * lower_slope,
        upper_cell - 0.5 * (1.0 + courant) * upper_slope,
    )


def zonal_change(quants, zonal_wind):
    courant = SPEED * (zonal_wind + jnp.roll(zonal_wind, -1, axis=-1))
    slopes = minmod(quants - jnp.roll(quants, 1, axis=-1), jnp.roll(quants, -1, axis=-1) - quants)
    face_value = upwind_face(
        quants, jnp.roll(quants, -1, axis=-1), slopes, jnp.roll(slopes, -1, axis=-1), courant
    )
    face_flux = courant * face_value
    return face_flux - jnp.roll(face_flux, 1, axis=-1)


def meridional_change(
    lower_cell, upper_cell, lower_slope, upper_slope, lower_wind, upper_wind, cos_face, cos_center
):
    courant = SPEED * (lower_wind + upper_wind)
    face_flux = (
        courant
        * cos_face[:, None]
        * upwind_face(lower_cell, upper_cell, lower_slope, upper_slope, courant)
    )
    return (face_flux[..., 1:, :] - face_flux[..., :-1, :]) / cos_center[:, None]


def center_cos(row_index):
    angle = ((row_index.astype(jnp.float32) + 0.5) * SPACING - 90.0) * (math.pi / 180.0)
    return jnp.cos(angle)


def face_cos(face_index):
    angle = (face_index.astype(jnp.float32) * SPACING - 90.0) * (math.pi / 180.0)
    return jnp.where(face_index == 0, 0.0, jnp.cos(angle))


def products(padded):
    return jnp.stack(
        [padded[0], padded[0] * padded[1], padded[0] * padded[2], padded[0] * padded[3]]
    )


def phase_tables(first_index, second_index, modulus):
    angle = (first_index[:, None] * second_index[None, :] % modulus).astype(jnp.float32) * (
        2.0 * math.pi / modulus
    )
    return (jnp.cos(angle), jnp.sin(angle))


def spectral_filter(field_block, cos_ratio):
    lon_count = field_block.shape[-1]
    inner_count = 1
    for divisor in range(1, lon_count + 1):
        if divisor * divisor <= lon_count and lon_count % divisor == 0:
            inner_count = divisor
    outer_count = lon_count // inner_count
    precise = lax.Precision.HIGHEST
    inner_index = jnp.arange(inner_count)
    outer_index = jnp.arange(outer_count)
    outer_cos, outer_sin = phase_tables(outer_index, outer_index, outer_count)
    inner_cos, inner_sin = phase_tables(inner_index, inner_index, inner_count)
    twist_cos, twist_sin = phase_tables(inner_index, outer_index, lon_count)
    wave_index = jnp.arange(lon_count)
    sine_wave = jnp.sin(wave_index.astype(jnp.float32) * (math.pi / lon_count))
    ratio_grid = cos_ratio[:, None]
    damping = (ratio_grid / jnp.maximum(sine_wave[None, :], ratio_grid)) ** 2 / lon_count
    damping = damping.reshape(damping.shape[0], inner_count, outer_count)
    lead = field_block.shape[:-1]
    samples = field_block.reshape(lead + (outer_count, inner_count))
    first_re = jnp.einsum("flabm,bk->flamk", samples, outer_cos, precision=precise)
    first_im = -jnp.einsum("flabm,bk->flamk", samples, outer_sin, precision=precise)
    turned_re = first_re * twist_cos + first_im * twist_sin
    turned_im = first_im * twist_cos - first_re * twist_sin
    spec_re = jnp.einsum("flamk,mj->flajk", turned_re, inner_cos, precision=precise) + jnp.einsum(
        "flamk,mj->flajk", turned_im, inner_sin, precision=precise
    )
    spec_im = jnp.einsum("flamk,mj->flajk", turned_im, inner_cos, precision=precise) - jnp.einsum(
        "flamk,mj->flajk", turned_re, inner_sin, precision=precise
    )
    spec_re = spec_re * damping
    spec_im = spec_im * damping
    back_re = jnp.einsum("flajk,mj->flamk", spec_re, inner_cos, precision=precise) - jnp.einsum(
        "flajk,mj->flamk", spec_im, inner_sin, precision=precise
    )
    back_im = jnp.einsum("flajk,mj->flamk", spec_im, inner_cos, precision=precise) + jnp.einsum(
        "flajk,mj->flamk", spec_re, inner_sin, precision=precise
    )
    untwist_re = back_re * twist_cos - back_im * twist_sin
    untwist_im = back_im * twist_cos + back_re * twist_sin
    rebuilt = jnp.einsum("flamk,kb->flabm", untwist_re, outer_cos, precision=precise) - jnp.einsum(
        "flamk,kb->flabm", untwist_im, outer_sin, precision=precise
    )
    return rebuilt.reshape(lead + (lon_count,))


def filter_if(needed, field_block, cos_ratio):

    def apply_filter(inner):
        return spectral_filter(inner, cos_ratio)

    def keep_rows(inner):
        return inner

    return lax.cond(needed, apply_filter, keep_rows, field_block)


def remap_columns(column_block, shares):
    level_count = column_block.shape[1]
    fields = column_block[:3]
    thick = column_block[3]
    upper_src = jnp.cumsum(thick, axis=0)
    lower_src = upper_src - thick
    column_total = upper_src[-1]
    target = column_total[None] * shares[:, None, None]
    upper_dst = column_total[None] * jnp.cumsum(shares)[:, None, None]
    lower_dst = upper_dst - target
    pieces = []
    for block_start in range(0, level_count, 8):
        block_top = upper_dst[block_start : block_start + 8]
        block_bottom = lower_dst[block_start : block_start + 8]
        intersection = jnp.maximum(
            0.0,
            jnp.minimum(block_top[:, None], upper_src[None])
            - jnp.maximum(block_bottom[:, None], lower_src[None]),
        )
        block_target = target[block_start : block_start + 8]
        remapped = [
            jnp.sum(intersection * fields[field_index][None], axis=1) / block_target
            for field_index in range(3)
        ]
        pieces.append(jnp.stack(remapped))
    all_fields = jnp.concatenate(pieces, axis=1)
    return jnp.concatenate([all_fields, target[None]], axis=0)


def on_device(
    zonal_velocity, meridional_velocity, heat_anomaly, layer_pressure_depth, reference_layer_shares
):
    band_index = lax.axis_index("lat")
    lat_rows = layer_pressure_depth.shape[1]
    row_index = band_index * lat_rows + jnp.arange(lat_rows)
    face_index = band_index * lat_rows + jnp.arange(lat_rows + 1)
    cos_center = center_cos(row_index)
    cos_face = face_cos(face_index)
    given_arrays = jnp.stack(
        [layer_pressure_depth, heat_anomaly, zonal_velocity, meridional_velocity]
    )
    padded = extended(given_arrays, (("lat", 2),), 2)
    quants = products(padded)
    wind_pad = padded[3]
    slopes = minmod(quants[:, :, 1:-1] - quants[:, :, :-2], quants[:, :, 2:] - quants[:, :, 1:-1])
    change_y = meridional_change(
        quants[:, :, 1:-2],
        quants[:, :, 2:-1],
        slopes[:, :, :-1],
        slopes[:, :, 1:],
        wind_pad[:, 1:-2],
        wind_pad[:, 2:-1],
        cos_face,
        cos_center,
    )
    own_quants = quants[:, :, 2:-2]
    own_wind = padded[2, :, 2:-2]
    updated = own_quants - zonal_change(own_quants, own_wind) - change_y
    fields = updated[1:] / updated[0]
    cos_ratio = cos_center / QUARTER
    polar_band = jnp.min(cos_center) < QUARTER
    smoothed = filter_if(polar_band, fields, cos_ratio)
    columns = jnp.concatenate([smoothed, updated[:1]], axis=0)
    shares = reference_layer_shares / jnp.sum(reference_layer_shares)
    fields_count, levels, rows, lon_count = columns.shape
    parts = lax.axis_size("lev")
    cut = jnp.stack(jnp.split(columns, parts, axis=3))
    moved = lax.all_to_all(cut, "lev", split_axis=0, concat_axis=0, tiled=True)
    moved = jnp.moveaxis(moved, 0, 1).reshape(
        fields_count, levels * parts, rows, lon_count // parts
    )
    result = remap_columns(moved, shares)
    return (result[0], result[1], result[2], result[3])


def solution(mesh):
    return jax.shard_map(
        on_device,
        mesh=mesh,
        in_specs=(
            P("lev", "lat", None),
            P("lev", "lat", None),
            P("lev", "lat", None),
            P("lev", "lat", None),
            P(),
        ),
        out_specs=(
            P(None, "lat", "lev"),
            P(None, "lat", "lev"),
            P(None, "lat", "lev"),
            P(None, "lat", "lev"),
        ),
        check_vma=False,
    )
```

```python
import math

import jax
import jax.numpy as jnp
import numpy as np
from jax import lax
from jax.experimental import pallas as pl
from jax.experimental.pallas import tpu as pltpu
from jax.sharding import PartitionSpec as P

SPEED = 0.04
QUARTER = math.cos(math.pi / 4.0)
SPACING = 180.0 / 1440.0
LON = 2880
ROWS = 4
LEVELS = 4
GROUPS = 4
COARSE = 12
FINE = 240
WIDE = 256
EDGE = 8
PER = COARSE // GROUPS
WAVES = COARSE // 2 + 1
MESH = pl.DeviceIdType.MESH


def grid_table(bands):
    f32 = np.float32
    rows = np.arange(bands * ROWS)
    faces = np.arange(bands * ROWS + 1)
    scale = f32(math.pi / 180.0)
    center = np.cos(((rows.astype(f32) + f32(0.5)) * f32(SPACING) - f32(90.0)) * scale)
    face = np.cos((faces.astype(f32) * f32(SPACING) - f32(90.0)) * scale)
    face = np.where(faces == 0, f32(0.0), face)
    table = np.zeros((bands, 16), f32)
    for band in range(bands):
        at = band * ROWS
        table[band, 0:4] = f32(1.0) / center[at : at + 4]
        table[band, 4:9] = face[at : at + 5]
        table[band, 9:13] = center[at : at + 4] / f32(QUARTER)
    return table


def split_bf16(array):
    high = array.astype(jnp.bfloat16)
    low = (array - high.astype(np.float32)).astype(jnp.bfloat16)
    return high, low


def constants():
    cell = np.arange(FINE)
    wave = np.arange(FINE)
    angle = 2.0 * np.pi * (np.outer(cell, wave) % FINE) / FINE
    cos, sin = np.cos(angle), np.sin(angle)
    forward = np.zeros((2 * WIDE, 2 * WIDE))
    spots = slice(EDGE, EDGE + FINE)
    spots_im = slice(WIDE + EDGE, WIDE + EDGE + FINE)
    forward[spots, 0:FINE] = cos
    forward[spots, WIDE : WIDE + FINE] = -sin
    forward[spots_im, 0:FINE] = sin
    forward[spots_im, WIDE : WIDE + FINE] = cos
    backward = np.zeros((2 * WIDE, 2 * WIDE))
    backward[0:FINE, spots] = cos.T
    backward[0:FINE, spots_im] = sin.T
    backward[WIDE : WIDE + FINE, spots] = -sin.T
    backward[WIDE : WIDE + FINE, spots_im] = cos.T
    matrices = np.stack(
        [m for whole in (forward, backward) for m in split_bf16(whole.astype(np.float32))]
    )
    tables = np.zeros((3, 8, WIDE), np.float32)
    for order in range(WAVES):
        turn = 2.0 * np.pi * order * cell / LON
        tables[0, order, spots] = np.cos(turn)
        tables[1, order, spots] = np.sin(turn)
        number = (order + COARSE * wave).astype(np.float32)
        tables[2, order, 0:FINE] = np.sin(number * np.float32(math.pi / LON))
    return matrices, tables


def cos_of(index):
    value = math.cos(2.0 * math.pi * index / COARSE)
    return round(value) if abs(value - round(value)) < 1e-9 else round(2 * value) / 2 if abs(
        2 * value - round(2 * value)
    ) < 1e-9 else value


def combine(terms):
    total = None
    for factor, array in terms:
        if factor == 0:
            continue
        if total is None:
            total = array if factor == 1 else -array if factor == -1 else factor * array
        elif factor == 1:
            total = total + array
        elif factor == -1:
            total = total - array
        else:
            total = total + factor * array
    return total


def forward_blocks(x):
    even = {n: x[n] + x[COARSE - n] for n in range(1, 6)}
    odd = {n: x[n] - x[COARSE - n] for n in range(1, 6)}
    ends = {0: x[0] + x[6], 1: x[0] - x[6]}
    even_sum = {n: even[n] + even[6 - n] for n in (1, 2)}
    even_dif = {n: even[n] - even[6 - n] for n in (1, 2)}
    odd_sum = {n: odd[n] + odd[6 - n] for n in (1, 2)}
    odd_dif = {n: odd[n] - odd[6 - n] for n in (1, 2)}
    real, imag = [], []
    for k in range(WAVES):
        pick = even_dif if k % 2 else even_sum
        terms = [(1, ends[k % 2])] + [(cos_of(n * k), pick[n]) for n in (1, 2)]
        terms.append((cos_of(3 * k), even[3]))
        real.append(combine(terms))
        if 0 < k < 6:
            pick = odd_sum if k % 2 else odd_dif
            terms = [(-cos_of(n * k - 3), pick[n]) for n in (1, 2)]
            terms.append((-cos_of(3 * k - 3), odd[3]))
            imag.append(combine(terms))
        else:
            imag.append(None)
    return real, imag


def backward_blocks(real, imag):
    base = {0: real[0] + real[6], 1: real[0] - real[6]}
    blocks = [None] * COARSE
    for b in range(0, 7):
        cosine = combine([(1, base[b % 2])] + [(cos_of(k * b), real[k]) for k in range(1, 6)])
        if b in (0, 6):
            blocks[b] = cosine
            continue
        sine = combine([(-cos_of(k * b - 3), imag[k]) for k in range(1, 6)])
        blocks[b] = cosine + sine
        blocks[COARSE - b] = cosine - sine
    return blocks


def minmod(left, right):
    return jnp.maximum(jnp.minimum(left, right), 0.0) + jnp.minimum(jnp.maximum(left, right), 0.0)


def window(load, block):
    lane = lax.broadcasted_iota(jnp.int32, (8, WIDE), 1)
    if block == 0:
        body = pltpu.roll(load(0, 256), EDGE, 1)
        tail = pltpu.roll(load(2688, 2944), 256 - (LON - EDGE - 2688), 1)
        return jnp.where(lane < EDGE, tail, body)
    start = FINE * block - EDGE
    first = start // 128 * 128
    body = pltpu.roll(load(first, first + 384), (384 - (start - first)) % 384, 1)[:, :WIDE]
    if block == COARSE - 1:
        head = pltpu.roll(load(0, 256), WIDE - EDGE, 1)
        body = jnp.where(lane >= WIDE - EDGE, head, body)
    return body


def kernel(
    grid_ref, share_ref, u_ref, v_ref, t_ref, h_ref, mat_ref, tab_ref,
    out_ref,
    raw, cut, field, sent, held, spread, gain, z_hi, z_lo, field_out,
    halo_send, halo_recv, turn_send, turn_recv, own_sem,
):
    bands = lax.axis_size("lat")
    band = lax.axis_index("lat")
    group = lax.axis_index("lev")
    above = (lax.rem(band + 1, bands), group)
    below = (lax.rem(band + bands - 1, bands), group)
    partners = [(band, lax.rem(group + step, GROUPS)) for step in range(1, GROUPS)]

    barrier = pltpu.get_barrier_semaphore()
    for device in [above, below] + partners:
        pl.semaphore_signal(barrier, inc=1, device_id=device, device_id_type=MESH)

    for row in range(ROWS):
        raw[0, 2 + row, 0:4, 0:LON] = h_ref[:, row, :]
        raw[0, 2 + row, 4:8, 0:LON] = v_ref[:, row, :]
        raw[1, 2 + row, 0:4, 0:LON] = u_ref[:, row, :]
        raw[1, 2 + row, 4:8, 0:LON] = t_ref[:, row, :]

    pl.semaphore_wait(barrier, 2 + len(partners))

    def halo(pair, side):
        return pltpu.make_async_remote_copy(
            src_ref=raw.at[pair, pl.ds(2 if side else 4, 2)],
            dst_ref=raw.at[pair, pl.ds(6 if side else 0, 2)],
            send_sem=halo_send.at[pair, side],
            recv_sem=halo_recv.at[pair, side],
            device_id=below if side else above,
            device_id_type=MESH,
        )

    halos = [halo(pair, side) for pair in range(2) for side in range(2)]
    for copy in halos:
        copy.start()

    def cut_row(pair, row):
        def load(first, last):
            return raw[pair, row, :, first:last]

        for block in range(COARSE):
            cut[pair, row, block] = window(load, block)

    def cut_own(step, carry):
        cut_row(step // ROWS, 2 + lax.rem(step, ROWS))
        return carry

    lax.fori_loop(0, 2 * ROWS, cut_own, 0)

    sub16 = lax.broadcasted_iota(jnp.int32, (16, WIDE), 0)
    ratio = jnp.full((16, WIDE), grid_ref[band, 9])
    for row in range(1, ROWS):
        ratio = jnp.where(sub16 >= LEVELS * row, grid_ref[band, 9 + row], ratio)
    for order in range(WAVES):
        sine = jnp.broadcast_to(tab_ref[2, order : order + 1, :], (16, WIDE))
        damping = ratio / jnp.maximum(sine, ratio)
        gain[order] = damping * damping * ((1.0 if order in (0, 6) else 2.0) / LON)

    for copy in halos:
        copy.wait_recv()

    def cut_halo(step, carry):
        row = lax.rem(step, 4)
        cut_row(step // 4, row + 4 * (row // 2))
        return carry

    lax.fori_loop(0, 8, cut_halo, 0)

    has_below = jnp.where(band > 0, 1.0, 0.0)
    has_above = jnp.where(band < bands - 1, 1.0, 0.0)

    def advect(block, carry):
        low = lax.broadcasted_iota(jnp.int32, (8, WIDE), 0) < 4

        def swap(array):
            return pltpu.roll(array, 4, 0)

        quants = ([], [])
        north, east = [], []
        for row in range(8):
            first, second = cut[0, row, block], cut[1, row, block]
            if row < 2:
                first, second = first * has_below, second * has_below
            elif row > 5:
                first, second = first * has_above, second * has_above
            turned = swap(first)
            thick = jnp.where(low, first, turned)
            north.append(jnp.where(low, turned, first))
            quants[0].append(jnp.where(low, first, first * thick))
            quants[1].append(second * thick)
            if 2 <= row < 6:
                east.append(jnp.where(low, second, swap(second)))

        rolled = lambda array, step: pltpu.roll(array, step % WIDE, 1)
        zonal_c = [SPEED * (wind + rolled(wind, -1)) for wind in east]
        face_c = [SPEED * (north[face + 1] + north[face + 2]) for face in range(5)]
        updated = ([], [])
        for pair in range(2):
            q = quants[pair]
            diff = [q[row + 1] - q[row] for row in range(7)]
            slope = [None] + [minmod(diff[row - 1], diff[row]) for row in range(1, 7)]
            flux = []
            for face in range(5):
                c = face_c[face]
                up = c >= 0.0
                value = jnp.where(up, q[face + 1], q[face + 2])
                lean = jnp.where(up, slope[face + 1], slope[face + 2])
                part = jnp.where(up, 0.5, -0.5) - 0.5 * c
                flux.append(c * grid_ref[band, 4 + face] * (value + part * lean))
            for row in range(ROWS):
                own = q[row + 2]
                c = zonal_c[row]
                after = rolled(own, -1)
                step = after - own
                tilt = minmod(rolled(step, 1), step)
                up = c >= 0.0
                value = jnp.where(up, own, after)
                lean = jnp.where(up, tilt, rolled(tilt, -1))
                part = jnp.where(up, 0.5, -0.5) - 0.5 * c
                through = c * (value + part * lean)
                change = (flux[row + 1] - flux[row]) * grid_ref[band, row]
                updated[pair].append(own - (through - rolled(through, 1)) - change)
        for half in range(2):
            rows = pl.ds(8 * half, 8)
            one, two = updated[0][2 * half], updated[0][2 * half + 1]
            thick = jnp.where(low, one, swap(two))
            sent[0, block, rows] = thick
            field[0, block, rows] = jnp.where(low, swap(one), two) / thick
            one, two = updated[1][2 * half], updated[1][2 * half + 1]
            field[1, block, rows] = jnp.where(low, one, swap(two)) / thick
            field[2, block, rows] = jnp.where(low, swap(one), two) / thick
        return carry

    lax.fori_loop(0, COARSE, advect, 0)

    def turn(item, step):
        target = lax.rem(group + step, GROUPS)
        return pltpu.make_async_remote_copy(
            src_ref=sent.at[item, pl.ds(PER * target, PER)],
            dst_ref=held.at[item, group],
            send_sem=turn_send.at[item, step - 1],
            recv_sem=turn_recv.at[item, step - 1],
            device_id=(band, target),
            device_id_type=MESH,
        )

    def keep(item):
        return pltpu.make_async_copy(
            sent.at[item, pl.ds(PER * group, PER)], held.at[item, group], own_sem.at[item]
        )

    def start_turn(item):
        for step in (2, 3, 1):
            turn(item, step).start()
        keep(item).start()

    start_turn(0)

    for item in range(3):
        for tile in range(2):
            lanes = pl.ds(128 * tile, 128)
            real, imag = forward_blocks([field[item, block, :, lanes] for block in range(COARSE)])
            for order in range(WAVES):
                cos = jnp.broadcast_to(tab_ref[0, order : order + 1, lanes], (16, 128))
                sin = jnp.broadcast_to(tab_ref[1, order : order + 1, lanes], (16, 128))
                if imag[order] is None:
                    parts = (real[order] * cos, -(real[order] * sin))
                else:
                    parts = (
                        real[order] * cos + imag[order] * sin,
                        imag[order] * cos - real[order] * sin,
                    )
                for side, part in enumerate(parts):
                    spot = (pl.ds(16 * order, 16), pl.ds(WIDE * side + 128 * tile, 128))
                    high = part.astype(jnp.bfloat16)
                    z_hi[spot] = high
                    z_lo[spot] = (part - high.astype(jnp.float32)).astype(jnp.bfloat16)

        def product(index):
            high, low = z_hi[...], z_lo[...]
            return (
                jnp.dot(high, mat_ref[index], preferred_element_type=jnp.float32)
                + jnp.dot(low, mat_ref[index], preferred_element_type=jnp.float32)
                + jnp.dot(high, mat_ref[index + 1], preferred_element_type=jnp.float32)
            )

        damping = gain[...].reshape(16 * WAVES, WIDE)
        waves = product(0) * jnp.concatenate([damping, damping], axis=1)
        high = waves.astype(jnp.bfloat16)
        z_hi[...] = high
        z_lo[...] = (waves - high.astype(jnp.float32)).astype(jnp.bfloat16)
        spread[...] = product(2)
        for tile in range(2):
            real, imag = [], []
            for order in range(WAVES):
                rows = pl.ds(16 * order, 16)
                lanes = pl.ds(128 * tile, 128)
                cos = jnp.broadcast_to(tab_ref[0, order : order + 1, lanes], (16, 128))
                sin = jnp.broadcast_to(tab_ref[1, order : order + 1, lanes], (16, 128))
                re = spread[rows, lanes]
                im = spread[rows, pl.ds(WIDE + 128 * tile, 128)]
                real.append(re * cos - im * sin)
                imag.append(im * cos + re * sin)
            for block, value in enumerate(backward_blocks(real, imag)):
                sent[1 + item, block, :, pl.ds(128 * tile, 128)] = value
        start_turn(1 + item)

    level = lax.broadcasted_iota(jnp.int32, (16, 128), 0)
    running = share_ref[0]
    share = jnp.full((16, 128), share_ref[0])
    top_share = share
    for target in range(1, 16):
        running = running + share_ref[target]
        share = jnp.where(level >= target, share_ref[target], share)
        top_share = jnp.where(level >= target, running, top_share)
    whole = jnp.full((16, 128), running)
    share = share / whole
    top_share = top_share / whole

    for item in range(4):
        for step in range(1, GROUPS):
            source = lax.rem(group + GROUPS - step, GROUPS)
            pltpu.make_async_remote_copy(
                src_ref=sent.at[item, pl.ds(0, PER)],
                dst_ref=held.at[item, source],
                send_sem=turn_send.at[item, step - 1],
                recv_sem=turn_recv.at[item, step - 1],
                device_id=(band, source),
                device_id_type=MESH,
            ).wait_recv()
        keep(item).wait()

    def remap(step, carry):
        block = step // 2
        lanes = pl.ds(pl.multiple_of(128 * lax.rem(step, 2), 128), 128)
        place = pl.ds(pl.multiple_of(128 * step, 128), 128)
        for row in range(ROWS):
            def source(item, index):
                at = LEVELS * row + index % LEVELS
                line = held[item, index // LEVELS, block, pl.ds(at, 1), lanes]
                return line

            total = source(0, 0)
            for index in range(1, 16):
                total = total + source(0, index)
            total = jnp.broadcast_to(total, (16, 128))
            target = total * share
            top = total * top_share
            bottom = top - target
            lower = jnp.zeros((1, 128), jnp.float32)
            sums = [jnp.zeros((16, 128), jnp.float32)] * 3
            for index in range(16):
                upper = lower + source(0, index)
                common = jnp.maximum(
                    jnp.minimum(top, jnp.broadcast_to(upper, (16, 128)))
                    - jnp.maximum(bottom, jnp.broadcast_to(lower, (16, 128))),
                    0.0,
                )
                sums = [
                    one + common * jnp.broadcast_to(source(1 + item, index), (16, 128))
                    for item, one in enumerate(sums)
                ]
                lower = upper
            inverse = 1.0 / target
            spread_out = [sums[2] * inverse, sums[1] * inverse, sums[0] * inverse, target]
            for item in range(4):
                field_out[item, row, :, place] = spread_out[item]
        return carry

    lax.fori_loop(0, 2 * PER, remap, 0)

    lane = lax.broadcasted_iota(jnp.int32, (16, PER * WIDE), 1)

    def pack(step, carry):
        item, row = step // ROWS, lax.rem(step, ROWS)
        wide = field_out[item, row]
        packed = pltpu.roll(wide, PER * WIDE - EDGE, 1)
        for block in range(1, PER):
            shift = EDGE + (WIDE - FINE) * block
            packed = jnp.where(
                lane >= FINE * block, pltpu.roll(wide, PER * WIDE - shift, 1), packed
            )
        out_ref[item, row] = packed[:, : LON // GROUPS]
        return carry

    lax.fori_loop(0, 4 * ROWS, pack, 0)

    for copy in halos:
        copy.wait_send()
    for item in range(4):
        for step in range(1, GROUPS):
            turn(item, step).wait_send()


def on_device(
    zonal_velocity, meridional_velocity, heat_anomaly, layer_pressure_depth, reference_layer_shares
):
    matrices, tables = constants()
    f32 = jnp.float32
    vmem = pl.BlockSpec(memory_space=pltpu.VMEM)
    smem = pl.BlockSpec(memory_space=pltpu.SMEM)
    size = 16 * WAVES
    result = pl.pallas_call(
        kernel,
        out_shape=jax.ShapeDtypeStruct((4, ROWS, 16, LON // GROUPS), f32),
        in_specs=[smem, smem] + [vmem] * 6,
        out_specs=vmem,
        scratch_shapes=[
            pltpu.VMEM((2, 8, 8, 2944), f32),
            pltpu.VMEM((2, 8, COARSE, 8, WIDE), f32),
            pltpu.VMEM((3, COARSE, 16, WIDE), f32),
            pltpu.VMEM((4, COARSE, 16, WIDE), f32),
            pltpu.VMEM((4, GROUPS, PER, 16, WIDE), f32),
            pltpu.VMEM((size, 2 * WIDE), f32),
            pltpu.VMEM((WAVES, 16, WIDE), f32),
            pltpu.VMEM((size, 2 * WIDE), jnp.bfloat16),
            pltpu.VMEM((size, 2 * WIDE), jnp.bfloat16),
            pltpu.VMEM((4, ROWS, 16, PER * WIDE), f32),
            pltpu.SemaphoreType.DMA((2, 2)),
            pltpu.SemaphoreType.DMA((2, 2)),
            pltpu.SemaphoreType.DMA((4, 3)),
            pltpu.SemaphoreType.DMA((4, 3)),
            pltpu.SemaphoreType.DMA((4,)),
        ],
        compiler_params=pltpu.CompilerParams(
            collective_id=0, has_side_effects=True, vmem_limit_bytes=40 << 20
        ),
        cost_estimate=pl.CostEstimate(
            flops=2_000_000_000, bytes_accessed=4_000_000, transcendentals=0
        ),
    )(
        jnp.asarray(grid_table(lax.axis_size("lat"))),
        reference_layer_shares,
        zonal_velocity,
        meridional_velocity,
        heat_anomaly,
        layer_pressure_depth,
        jnp.asarray(matrices),
        jnp.asarray(tables),
    )
    result = jnp.transpose(result, (0, 2, 1, 3))
    return (result[0], result[1], result[2], result[3])


def solution(mesh):
    return jax.shard_map(
        on_device,
        mesh=mesh,
        in_specs=(
            P("lev", "lat", None),
            P("lev", "lat", None),
            P("lev", "lat", None),
            P("lev", "lat", None),
            P(),
        ),
        out_specs=(
            P(None, "lat", "lev"),
            P(None, "lat", "lev"),
            P(None, "lat", "lev"),
            P(None, "lat", "lev"),
        ),
        check_vma=False,
    )
```

```python
import math

import jax
import jax.numpy as jnp
import numpy as np
from jax import lax
from jax.experimental import pallas as pl
from jax.experimental.pallas import tpu as pltpu
from jax.sharding import PartitionSpec as P

SPEED = 0.04
QUARTER = math.cos(math.pi / 4.0)
SPACING = 180.0 / 1440.0
LON = 2880
ROWS = 4
LEVELS = 4
GROUPS = 4
COARSE = 12
FINE = 240
WIDE = 256
EDGE = 8
PER = COARSE // GROUPS
WAVES = COARSE // 2 + 1
MESH = pl.DeviceIdType.MESH


def grid_table(bands):
    f32 = np.float32
    rows = np.arange(bands * ROWS)
    faces = np.arange(bands * ROWS + 1)
    scale = f32(math.pi / 180.0)
    center = np.cos(((rows.astype(f32) + f32(0.5)) * f32(SPACING) - f32(90.0)) * scale)
    face = np.cos((faces.astype(f32) * f32(SPACING) - f32(90.0)) * scale)
    face = np.where(faces == 0, f32(0.0), face)
    table = np.zeros((bands, 4, 8, 128), f32)
    for sub in range(8):
        row = ROWS * np.arange(bands) + sub % ROWS
        table[:, 0, sub] = (f32(1.0) / center[row])[:, None]
        table[:, 1, sub] = face[row + 1][:, None]
        outer = ROWS * np.arange(bands) + (0 if sub % ROWS < 2 else ROWS)
        table[:, 2, sub] = face[outer][:, None]
        table[:, 3, sub] = (center[row] / f32(QUARTER))[:, None]
    return table


def split_bf16(array):
    high = array.astype(jnp.bfloat16)
    low = (array - high.astype(np.float32)).astype(jnp.bfloat16)
    return high, low


def constants():
    cell = np.arange(FINE)
    wave = np.arange(FINE)
    angle = 2.0 * np.pi * (np.outer(cell, wave) % FINE) / FINE
    cos, sin = np.cos(angle), np.sin(angle)
    forward = np.zeros((2 * WIDE, 2 * WIDE))
    spots = slice(EDGE, EDGE + FINE)
    spots_im = slice(WIDE + EDGE, WIDE + EDGE + FINE)
    forward[spots, 0:FINE] = cos
    forward[spots, WIDE : WIDE + FINE] = -sin
    forward[spots_im, 0:FINE] = sin
    forward[spots_im, WIDE : WIDE + FINE] = cos
    backward = np.zeros((2 * WIDE, 2 * WIDE))
    backward[0:FINE, spots] = cos.T
    backward[0:FINE, spots_im] = sin.T
    backward[WIDE : WIDE + FINE, spots] = -sin.T
    backward[WIDE : WIDE + FINE, spots_im] = cos.T
    matrices = np.stack(
        [m for whole in (forward, backward) for m in split_bf16(whole.astype(np.float32))]
    )
    tables = np.zeros((3, 8, WIDE), np.float32)
    for order in range(WAVES):
        turn = 2.0 * np.pi * order * cell / LON
        tables[0, order, spots] = np.cos(turn)
        tables[1, order, spots] = np.sin(turn)
        number = (order + COARSE * wave).astype(np.float32)
        tables[2, order, 0:FINE] = np.sin(number * np.float32(math.pi / LON))
    return matrices, tables


def cos_of(index):
    value = math.cos(2.0 * math.pi * index / COARSE)
    return round(value) if abs(value - round(value)) < 1e-9 else round(2 * value) / 2 if abs(
        2 * value - round(2 * value)
    ) < 1e-9 else value


def combine(terms):
    total = None
    for factor, array in terms:
        if factor == 0:
            continue
        if total is None:
            total = array if factor == 1 else -array if factor == -1 else factor * array
        elif factor == 1:
            total = total + array
        elif factor == -1:
            total = total - array
        else:
            total = total + factor * array
    return total


def forward_blocks(x):
    even = {n: x[n] + x[COARSE - n] for n in range(1, 6)}
    odd = {n: x[n] - x[COARSE - n] for n in range(1, 6)}
    ends = {0: x[0] + x[6], 1: x[0] - x[6]}
    even_sum = {n: even[n] + even[6 - n] for n in (1, 2)}
    even_dif = {n: even[n] - even[6 - n] for n in (1, 2)}
    odd_sum = {n: odd[n] + odd[6 - n] for n in (1, 2)}
    odd_dif = {n: odd[n] - odd[6 - n] for n in (1, 2)}
    real, imag = [], []
    for k in range(WAVES):
        pick = even_dif if k % 2 else even_sum
        terms = [(1, ends[k % 2])] + [(cos_of(n * k), pick[n]) for n in (1, 2)]
        terms.append((cos_of(3 * k), even[3]))
        real.append(combine(terms))
        if 0 < k < 6:
            pick = odd_sum if k % 2 else odd_dif
            terms = [(-cos_of(n * k - 3), pick[n]) for n in (1, 2)]
            terms.append((-cos_of(3 * k - 3), odd[3]))
            imag.append(combine(terms))
        else:
            imag.append(None)
    return real, imag


def backward_blocks(real, imag):
    base = {0: real[0] + real[6], 1: real[0] - real[6]}
    blocks = [None] * COARSE
    for b in range(0, 7):
        cosine = combine([(1, base[b % 2])] + [(cos_of(k * b), real[k]) for k in range(1, 6)])
        if b in (0, 6):
            blocks[b] = cosine
            continue
        sine = combine([(-cos_of(k * b - 3), imag[k]) for k in range(1, 6)])
        blocks[b] = cosine + sine
        blocks[COARSE - b] = cosine - sine
    return blocks


def minmod(left, right):
    return jnp.maximum(jnp.minimum(left, right), 0.0) + jnp.minimum(jnp.maximum(left, right), 0.0)


def window(load, block):
    lane = lax.broadcasted_iota(jnp.int32, (8, WIDE), 1)
    if block == 0:
        body = pltpu.roll(load(0, 256), EDGE, 1)
        tail = pltpu.roll(load(2816, LON), 128 - (LON - EDGE - 2816), 1)
        return jnp.concatenate(
            [jnp.where(lane[:, :128] < EDGE, tail, body[:, :128]), body[:, 128:]], axis=1
        )
    start = FINE * block - EDGE
    first = start // 128 * 128
    body = pltpu.roll(load(first, first + 384), (384 - (start - first)) % 384, 1)[:, :WIDE]
    if block == COARSE - 1:
        head = pltpu.roll(load(0, 256), WIDE - EDGE, 1)
        body = jnp.where(lane >= WIDE - EDGE, head, body)
    return body


def limits(courant):
    return jnp.where(courant >= 0.0, 0.5, -0.5) - 0.5 * courant


def kernel(
    grid_hbm, share_hbm, u_hbm, v_hbm, t_hbm, h_hbm, mat_hbm, tab_hbm,
    out_ref,
    given, mat_ref, tab_ref, grid_ref, share_ref,
    own, to_up, to_down, from_down, from_up, base, lean_ref, inverse_h,
    field, sent, held, spread, gain, z_hi, z_lo, weight, wide, target_ref,
    in_sem, halo_send, halo_recv, turn_send, turn_recv, own_sem,
):
    bands = lax.axis_size("lat")
    band = lax.axis_index("lat")
    group = lax.axis_index("lev")
    above = (lax.rem(band + 1, bands), group)
    below = (lax.rem(band + bands - 1, bands), group)
    partners = [(band, lax.rem(group + step, GROUPS)) for step in range(1, GROUPS)]

    barrier = pltpu.get_barrier_semaphore()
    for device in [above, below] + partners:
        pl.semaphore_signal(barrier, inc=1, device_id=device, device_id_type=MESH)

    loads = [
        pltpu.make_async_copy(source, given.at[item], in_sem.at[item])
        for item, source in enumerate((h_hbm, v_hbm, u_hbm, t_hbm))
    ]
    tables = [
        pltpu.make_async_copy(grid_hbm.at[band], grid_ref, in_sem.at[4]),
        pltpu.make_async_copy(tab_hbm, tab_ref, in_sem.at[5]),
        pltpu.make_async_copy(share_hbm, share_ref, in_sem.at[6]),
        pltpu.make_async_copy(mat_hbm, mat_ref, in_sem.at[7]),
    ]
    for copy in loads + tables:
        copy.start()

    def sub_row(shape):
        return lax.rem(lax.broadcasted_iota(jnp.int32, shape, 0), ROWS)

    place = sub_row((8, WIDE))

    def down(array, step):
        return pltpu.roll(array, step % 8, 0)

    def side(array, step):
        return pltpu.roll(array, step % WIDE, 1)

    def cut_item(item):
        for pair in range(2):

            def load(first, last):
                value = given[item, 2 * pair : 2 * pair + 2, :, first : min(last, LON)]
                value = value.reshape(8, min(last, LON) - first)
                short = -value.shape[1] % 128
                if short:
                    value = jnp.concatenate([value, jnp.zeros((8, short), jnp.float32)], axis=1)
                return value

            for block in range(COARSE):
                own[item, block, pair] = window(load, block)

        def edges(block, carry):
            a, b = own[item, block, 0], own[item, block, 1]
            to_up[item, block] = jnp.where(
                place < 2,
                jnp.where(place == 0, down(a, -3), down(b, -2)),
                jnp.where(place == 2, a, down(b, 1)),
            )
            to_down[item, block] = jnp.where(
                place < 2,
                jnp.where(place == 0, down(b, -1), a),
                jnp.where(place == 2, down(b, 2), down(a, 3)),
            )
            return carry

        lax.fori_loop(0, COARSE, edges, 0)

    def halo(item, way):
        return pltpu.make_async_remote_copy(
            src_ref=(to_down if way else to_up).at[item],
            dst_ref=(from_up if way else from_down).at[item],
            send_sem=halo_send.at[item, way],
            recv_sem=halo_recv.at[item, way],
            device_id=below if way else above,
            device_id_type=MESH,
        )

    halos = [halo(item, way) for item in range(4) for way in range(2)]
    for item in range(4):
        loads[item].wait()
        cut_item(item)
        if item == 0:
            pl.semaphore_wait(barrier, 2 + len(partners))
        for way in range(2):
            halo(item, way).start()
    for copy in tables:
        copy.wait()

    def zonal(block, carry):
        for pair in range(2):
            wind = own[2, block, pair]
            thick = own[0, block, pair]
            c = SPEED * (wind + side(wind, -1))
            up = c >= 0.0
            part = limits(c)
            for item in range(4):
                q = thick if item == 0 else thick * own[item, block, pair]
                after = side(q, -1)
                step = after - q
                tilt = minmod(side(step, 1), step)
                through = c * (
                    jnp.where(up, q, after) + part * jnp.where(up, tilt, side(tilt, -1))
                )
                base[item, block, pair] = q - (through - side(through, 1))
        return carry

    lax.fori_loop(0, COARSE, zonal, 0)

    ratio = jnp.concatenate([grid_ref[3], grid_ref[3]], axis=1)
    for order in range(WAVES):
        sine = jnp.broadcast_to(tab_ref[2, order : order + 1, :], (8, WIDE))
        damping = ratio / jnp.maximum(sine, ratio)
        damping = damping * damping * ((1.0 if order in (0, 6) else 2.0) / LON)
        gain[16 * order : 16 * order + 8] = damping
        gain[16 * order + 8 : 16 * order + 16] = damping

    has_below = jnp.where(band > 0, 1.0, 0.0)
    has_above = jnp.where(band < bands - 1, 1.0, 0.0)

    def outer(a, b):
        return jnp.where(
            place == 1, down(b, 1), jnp.where(place == 2, down(b, -1), a)
        )

    def wide_grid(index):
        return jnp.concatenate([grid_ref[index], grid_ref[index]], axis=1)

    def slants(block, carry):
        a, b = own[1, block, 0], own[1, block, 1]
        near = jnp.where(place < 2, from_down[1, block] * has_below, from_up[1, block] * has_above)
        winds = (a + down(a, -1), b + down(b, -1), near + outer(a, b))
        for index, wind in enumerate(winds):
            c = SPEED * wind
            lean_ref[block, 2 * index] = c * wide_grid(2 if index == 2 else 1)
            lean_ref[block, 2 * index + 1] = limits(c)
        return carry

    def meridional(item):
        def one(block, carry):
            sign = jnp.where(place < 2, 1.0, -1.0)
            low, high = from_down[0, block] * has_below, from_up[0, block] * has_above
            cells = [own[0, block, 0], own[0, block, 1]]
            if item:
                low, high = low * from_down[item, block], high * from_up[item, block]
                cells = [cells[pair] * own[item, block, pair] for pair in range(2)]
            near = jnp.where(place < 2, low, high)
            far = jnp.where(place < 2, down(low, -2), down(high, 2))
            edge = outer(*cells)
            gap = edge - near
            near_slope = sign * minmod(near - far, gap)
            gap = sign * gap
            slopes, flows = [], []
            for pair in range(2):
                x = cells[pair]
                after = down(x, -1)
                inner = after - x
                upper = jnp.where(place == 3, down(gap, 1) if pair else gap, inner)
                lower = jnp.where(place == 0, down(gap, -1) if pair else gap, down(inner, 1))
                slope = minmod(lower, upper)
                slopes.append(slope)
                part = lean_ref[block, 2 * pair + 1]
                up = part > 0.0
                flows.append(
                    lean_ref[block, 2 * pair]
                    * (jnp.where(up, x, after) + part * jnp.where(up, slope, down(slope, -1)))
                )
            part = lean_ref[block, 5]
            pick = part * sign > 0.0
            flow = lean_ref[block, 4] * (
                jnp.where(pick, near, edge) + part * jnp.where(pick, near_slope, outer(*slopes))
            )
            for pair in range(2):
                above_flow = jnp.where(place == 3, down(flow, 1) if pair else flow, flows[pair])
                below_flow = jnp.where(
                    place == 0, down(flow, -1) if pair else flow, down(flows[pair], 1)
                )
                value = base[item, block, pair] - (above_flow - below_flow) * wide_grid(0)
                rows = pl.ds(8 * pair, 8)
                if item == 0:
                    sent[0, block, rows] = value
                    inverse_h[block, rows] = 1.0 / value
                else:
                    field[block, rows] = value * inverse_h[block, rows]
            return carry

        lax.fori_loop(0, COARSE, one, 0)

    def turn(item, step):
        target = lax.rem(group + step, GROUPS)
        return pltpu.make_async_remote_copy(
            src_ref=sent.at[item, pl.ds(PER * target, PER)],
            dst_ref=held.at[item, group],
            send_sem=turn_send.at[item, step - 1],
            recv_sem=turn_recv.at[item, step - 1],
            device_id=(band, target),
            device_id_type=MESH,
        )

    def keep(item):
        return pltpu.make_async_copy(
            sent.at[item, pl.ds(PER * group, PER)], held.at[item, group], own_sem.at[item]
        )

    def start_turn(item):
        for step in (2, 3, 1):
            turn(item, step).start()
        keep(item).start()

    def end_turn(item):
        for step in range(1, GROUPS):
            source = lax.rem(group + GROUPS - step, GROUPS)
            pltpu.make_async_remote_copy(
                src_ref=sent.at[item, pl.ds(0, PER)],
                dst_ref=held.at[item, source],
                send_sem=turn_send.at[item, step - 1],
                recv_sem=turn_recv.at[item, step - 1],
                device_id=(band, source),
                device_id_type=MESH,
            ).wait_recv()
        keep(item).wait()

    def product(index):
        high, low = z_hi[...], z_lo[...]
        return (
            jnp.dot(high, mat_ref[index], preferred_element_type=jnp.float32)
            + jnp.dot(low, mat_ref[index], preferred_element_type=jnp.float32)
            + jnp.dot(high, mat_ref[index + 1], preferred_element_type=jnp.float32)
        )

    def polar(item):
        def forward(tile, carry):
            lanes = pl.ds(pl.multiple_of(128 * tile, 128), 128)
            real, imag = forward_blocks([field[block, :, lanes] for block in range(COARSE)])
            for order in range(WAVES):
                cos = jnp.broadcast_to(tab_ref[0, order : order + 1, lanes], (16, 128))
                sin = jnp.broadcast_to(tab_ref[1, order : order + 1, lanes], (16, 128))
                if imag[order] is None:
                    parts = (real[order] * cos, -(real[order] * sin))
                else:
                    parts = (
                        real[order] * cos + imag[order] * sin,
                        imag[order] * cos - real[order] * sin,
                    )
                for half, part in enumerate(parts):
                    at = pl.multiple_of(WIDE * half + 128 * tile, 128)
                    spot = (pl.ds(16 * order, 16), pl.ds(at, 128))
                    high = part.astype(jnp.bfloat16)
                    z_hi[spot] = high
                    z_lo[spot] = (part - high.astype(jnp.float32)).astype(jnp.bfloat16)
            return carry

        lax.fori_loop(0, 2, forward, 0)
        damping = gain[...]
        waves = product(0) * jnp.concatenate([damping, damping], axis=1)
        high = waves.astype(jnp.bfloat16)
        z_hi[...] = high
        z_lo[...] = (waves - high.astype(jnp.float32)).astype(jnp.bfloat16)
        spread[...] = product(2)

        def backward(tile, carry):
            lanes = pl.ds(pl.multiple_of(128 * tile, 128), 128)
            other = pl.ds(pl.multiple_of(WIDE + 128 * tile, 128), 128)
            real, imag = [], []
            for order in range(WAVES):
                rows = pl.ds(16 * order, 16)
                cos = jnp.broadcast_to(tab_ref[0, order : order + 1, lanes], (16, 128))
                sin = jnp.broadcast_to(tab_ref[1, order : order + 1, lanes], (16, 128))
                re, im = spread[rows, lanes], spread[rows, other]
                real.append(re * cos - im * sin)
                imag.append(im * cos + re * sin)
            for block, value in enumerate(backward_blocks(real, imag)):
                sent[item, block, :, lanes] = value
            return carry

        lax.fori_loop(0, 2, backward, 0)

    def end_halo(item):
        for way in range(2):
            halo(item, way).wait_recv()

    end_halo(0)
    end_halo(1)
    lax.fori_loop(0, COARSE, slants, 0)
    meridional(0)
    start_turn(0)
    for item in range(1, 4):
        if item > 1:
            end_halo(item)
        meridional(item)
        polar(item)
        start_turn(item)

    first_half = lax.broadcasted_iota(jnp.int32, (8, 128), 0) < ROWS

    def lines(item, block, lanes):
        found = []
        for index in range(8):
            both = held[item, index // 2, block, pl.ds(8 * (index % 2), 8), lanes]
            turned = down(both, ROWS)
            found.append(jnp.where(first_half, both, turned))
            found.append(jnp.where(first_half, turned, both))
        return found

    def tile_of(step):
        return step // 2, pl.ds(pl.multiple_of(128 * lax.rem(step, 2), 128), 128)

    def weigh(step, carry):
        uppers = []
        for line in lines(0, *tile_of(step)):
            uppers.append(uppers[-1] + line if uppers else line)
        total = uppers[-1]
        lowers = [jnp.zeros((8, 128), jnp.float32)] + uppers[:-1]
        running = share_ref[0]
        for level in range(1, 16):
            running = running + share_ref[level]
        unit = total / jnp.full((8, 128), running)
        running = jnp.float32(0.0)
        for pair in range(8):
            one, two = share_ref[2 * pair], share_ref[2 * pair + 1]
            target = unit * jnp.where(first_half, one, two)
            top = unit * jnp.where(first_half, running + one, running + one + two)
            running = running + one + two
            bottom = top - target
            wide[pair, step] = target
            target_ref[step, pair] = 1.0 / target
            for index in range(16):
                weight[step, pair, index] = jnp.maximum(
                    jnp.minimum(top, uppers[index]) - jnp.maximum(bottom, lowers[index]), 0.0
                )
        return carry

    def gather(item):
        def one(step, carry):
            found = lines(item, *tile_of(step))
            for pair in range(8):
                total = weight[step, pair, 0] * found[0]
                for index in range(1, 16):
                    total = total + weight[step, pair, index] * found[index]
                wide[pair, step] = total * target_ref[step, pair]
            return carry

        lax.fori_loop(0, 2 * PER, one, 0)

    def pack(output):
        def one(pair, carry):
            lane = lax.broadcasted_iota(jnp.int32, (8, 128), 1)
            shifts = (128 - EDGE, 104, 88)
            t = [pltpu.roll(wide[pair, step], shifts[step // 2], 1) for step in range(6)]
            tiles = [
                jnp.where(lane < 120, t[0], t[1]),
                jnp.where(lane < 112, t[1], t[2]),
                jnp.where(lane < 104, t[2], t[3]),
                jnp.where(lane < 96, t[3], t[4]),
                jnp.where(lane < 88, t[4], t[5]),
                t[5],
            ]
            for at, tile in enumerate(tiles):
                size = min(128, LON // GROUPS - 128 * at)
                value = tile[:, :size].reshape(2, ROWS, size)
                out_ref[output, pl.ds(2 * pair, 2), :, 128 * at : 128 * at + size] = value
            return carry

        lax.fori_loop(0, 8, one, 0)

    end_turn(0)
    lax.fori_loop(0, 2 * PER, weigh, 0)
    pack(3)
    for item in range(1, 4):
        end_turn(item)
        gather(item)
        pack((0, 2, 1, 0)[item])

    for copy in halos:
        copy.wait_send()
    for item in range(4):
        for step in range(1, GROUPS):
            turn(item, step).wait_send()


def on_device(
    zonal_velocity, meridional_velocity, heat_anomaly, layer_pressure_depth, reference_layer_shares
):
    matrices, tables = constants()
    f32 = jnp.float32
    hbm = pl.BlockSpec(memory_space=pl.ANY)
    size = 16 * WAVES
    result = pl.pallas_call(
        kernel,
        out_shape=jax.ShapeDtypeStruct((4, 16, ROWS, LON // GROUPS), f32),
        in_specs=[hbm] * 8,
        out_specs=pl.BlockSpec(memory_space=pltpu.VMEM),
        scratch_shapes=[
            pltpu.VMEM((4, LEVELS, ROWS, LON), f32),
            pltpu.VMEM((4, 2 * WIDE, 2 * WIDE), jnp.bfloat16),
            pltpu.VMEM((3, 8, WIDE), f32),
            pltpu.VMEM((4, 8, 128), f32),
            pltpu.SMEM((16,), f32),
            pltpu.VMEM((4, COARSE, 2, 8, WIDE), f32),
            pltpu.VMEM((4, COARSE, 8, WIDE), f32),
            pltpu.VMEM((4, COARSE, 8, WIDE), f32),
            pltpu.VMEM((4, COARSE, 8, WIDE), f32),
            pltpu.VMEM((4, COARSE, 8, WIDE), f32),
            pltpu.VMEM((4, COARSE, 2, 8, WIDE), f32),
            pltpu.VMEM((COARSE, 6, 8, WIDE), f32),
            pltpu.VMEM((COARSE, 16, WIDE), f32),
            pltpu.VMEM((COARSE, 16, WIDE), f32),
            pltpu.VMEM((4, COARSE, 16, WIDE), f32),
            pltpu.VMEM((4, GROUPS, PER, 16, WIDE), f32),
            pltpu.VMEM((size, 2 * WIDE), f32),
            pltpu.VMEM((size, WIDE), f32),
            pltpu.VMEM((size, 2 * WIDE), jnp.bfloat16),
            pltpu.VMEM((size, 2 * WIDE), jnp.bfloat16),
            pltpu.VMEM((2 * PER, 8, 16, 8, 128), f32),
            pltpu.VMEM((8, 2 * PER, 8, 128), f32),
            pltpu.VMEM((2 * PER, 8, 8, 128), f32),
            pltpu.SemaphoreType.DMA((8,)),
            pltpu.SemaphoreType.DMA((4, 2)),
            pltpu.SemaphoreType.DMA((4, 2)),
            pltpu.SemaphoreType.DMA((4, 3)),
            pltpu.SemaphoreType.DMA((4, 3)),
            pltpu.SemaphoreType.DMA((4,)),
        ],
        compiler_params=pltpu.CompilerParams(
            collective_id=0, has_side_effects=True, vmem_limit_bytes=56 << 20
        ),
        cost_estimate=pl.CostEstimate(
            flops=2_000_000_000, bytes_accessed=4_000_000, transcendentals=0
        ),
    )(
        jnp.asarray(grid_table(lax.axis_size("lat"))),
        reference_layer_shares,
        zonal_velocity,
        meridional_velocity,
        heat_anomaly,
        layer_pressure_depth,
        jnp.asarray(matrices),
        jnp.asarray(tables),
    )
    return (result[0], result[1], result[2], result[3])


def solution(mesh):
    return jax.shard_map(
        on_device,
        mesh=mesh,
        in_specs=(
            P("lev", "lat", None),
            P("lev", "lat", None),
            P("lev", "lat", None),
            P("lev", "lat", None),
            P(),
        ),
        out_specs=(
            P(None, "lat", "lev"),
            P(None, "lat", "lev"),
            P(None, "lat", "lev"),
            P(None, "lat", "lev"),
        ),
        check_vma=False,
    )
```

```python
import math

import jax
import jax.numpy as jnp
import numpy as np
from jax import lax
from jax.experimental import pallas as pl
from jax.experimental.pallas import tpu as pltpu
from jax.sharding import PartitionSpec as P

SPEED = 0.04
QUARTER = math.cos(math.pi / 4.0)
SPACING = 180.0 / 1440.0
LON = 2880
ROWS = 4
LEVELS = 4
GROUPS = 4
COARSE = 12
FINE = 240
WIDE = 256
EDGE = 8
PER = COARSE // GROUPS
WAVES = COARSE // 2 + 1
MESH = pl.DeviceIdType.MESH


def grid_table(bands):
    f32 = np.float32
    rows = np.arange(bands * ROWS)
    faces = np.arange(bands * ROWS + 1)
    scale = f32(math.pi / 180.0)
    center = np.cos(((rows.astype(f32) + f32(0.5)) * f32(SPACING) - f32(90.0)) * scale)
    face = np.cos((faces.astype(f32) * f32(SPACING) - f32(90.0)) * scale)
    face = np.where(faces == 0, f32(0.0), face)
    table = np.zeros((bands, 4, 8, 128), f32)
    for sub in range(8):
        row = ROWS * np.arange(bands) + sub % ROWS
        table[:, 0, sub] = (f32(1.0) / center[row])[:, None]
        table[:, 1, sub] = face[row + 1][:, None]
        outer = ROWS * np.arange(bands) + (0 if sub % ROWS < 2 else ROWS)
        table[:, 2, sub] = face[outer][:, None]
        table[:, 3, sub] = (center[row] / f32(QUARTER))[:, None]
    return table


def split_bf16(array):
    high = array.astype(jnp.bfloat16)
    low = (array - high.astype(np.float32)).astype(jnp.bfloat16)
    return high, low


def constants():
    cell = np.arange(FINE)
    wave = np.arange(FINE)
    angle = 2.0 * np.pi * (np.outer(cell, wave) % FINE) / FINE
    cos, sin = np.cos(angle), np.sin(angle)
    forward = np.zeros((2 * WIDE, 2 * WIDE))
    spots = slice(EDGE, EDGE + FINE)
    spots_im = slice(WIDE + EDGE, WIDE + EDGE + FINE)
    forward[spots, 0:FINE] = cos
    forward[spots, WIDE : WIDE + FINE] = -sin
    forward[spots_im, 0:FINE] = sin
    forward[spots_im, WIDE : WIDE + FINE] = cos
    backward = np.zeros((2 * WIDE, 2 * WIDE))
    backward[0:FINE, spots] = cos.T
    backward[0:FINE, spots_im] = sin.T
    backward[WIDE : WIDE + FINE, spots] = -sin.T
    backward[WIDE : WIDE + FINE, spots_im] = cos.T
    matrices = np.stack(
        [m for whole in (forward, backward) for m in split_bf16(whole.astype(np.float32))]
    )
    tables = np.zeros((3, 8, WIDE), np.float32)
    for order in range(WAVES):
        turn = 2.0 * np.pi * order * cell / LON
        tables[0, order, spots] = np.cos(turn)
        tables[1, order, spots] = np.sin(turn)
        number = (order + COARSE * wave).astype(np.float32)
        tables[2, order, 0:FINE] = np.sin(number * np.float32(math.pi / LON))
    return matrices, tables


def cos_of(index):
    value = math.cos(2.0 * math.pi * index / COARSE)
    return round(value) if abs(value - round(value)) < 1e-9 else round(2 * value) / 2 if abs(
        2 * value - round(2 * value)
    ) < 1e-9 else value


def combine(terms):
    total = None
    for factor, array in terms:
        if factor == 0:
            continue
        if total is None:
            total = array if factor == 1 else -array if factor == -1 else factor * array
        elif factor == 1:
            total = total + array
        elif factor == -1:
            total = total - array
        else:
            total = total + factor * array
    return total


def forward_blocks(x):
    even = {n: x[n] + x[COARSE - n] for n in range(1, 6)}
    odd = {n: x[n] - x[COARSE - n] for n in range(1, 6)}
    ends = {0: x[0] + x[6], 1: x[0] - x[6]}
    even_sum = {n: even[n] + even[6 - n] for n in (1, 2)}
    even_dif = {n: even[n] - even[6 - n] for n in (1, 2)}
    odd_sum = {n: odd[n] + odd[6 - n] for n in (1, 2)}
    odd_dif = {n: odd[n] - odd[6 - n] for n in (1, 2)}
    real, imag = [], []
    for k in range(WAVES):
        pick = even_dif if k % 2 else even_sum
        terms = [(1, ends[k % 2])] + [(cos_of(n * k), pick[n]) for n in (1, 2)]
        terms.append((cos_of(3 * k), even[3]))
        real.append(combine(terms))
        if 0 < k < 6:
            pick = odd_sum if k % 2 else odd_dif
            terms = [(-cos_of(n * k - 3), pick[n]) for n in (1, 2)]
            terms.append((-cos_of(3 * k - 3), odd[3]))
            imag.append(combine(terms))
        else:
            imag.append(None)
    return real, imag


def backward_blocks(real, imag):
    base = {0: real[0] + real[6], 1: real[0] - real[6]}
    blocks = [None] * COARSE
    for b in range(0, 7):
        cosine = combine([(1, base[b % 2])] + [(cos_of(k * b), real[k]) for k in range(1, 6)])
        if b in (0, 6):
            blocks[b] = cosine
            continue
        sine = combine([(-cos_of(k * b - 3), imag[k]) for k in range(1, 6)])
        blocks[b] = cosine + sine
        blocks[COARSE - b] = cosine - sine
    return blocks


def minmod(left, right):
    return jnp.maximum(jnp.minimum(left, right), 0.0) + jnp.minimum(jnp.maximum(left, right), 0.0)


def window(load, block):
    lane = lax.broadcasted_iota(jnp.int32, (8, WIDE), 1)
    if block == 0:
        body = pltpu.roll(load(0, 256), EDGE, 1)
        tail = pltpu.roll(load(2816, LON), 128 - (LON - EDGE - 2816), 1)
        return jnp.concatenate(
            [jnp.where(lane[:, :128] < EDGE, tail, body[:, :128]), body[:, 128:]], axis=1
        )
    start = FINE * block - EDGE
    first = start // 128 * 128
    body = pltpu.roll(load(first, first + 384), (384 - (start - first)) % 384, 1)[:, :WIDE]
    if block == COARSE - 1:
        head = pltpu.roll(load(0, 256), WIDE - EDGE, 1)
        body = jnp.where(lane >= WIDE - EDGE, head, body)
    return body


def limits(courant):
    return jnp.where(courant >= 0.0, 0.5, -0.5) - 0.5 * courant


def kernel(
    grid_hbm, share_hbm, u_hbm, v_hbm, t_hbm, h_hbm, mat_hbm, tab_hbm,
    out_ref,
    given, mat_ref, tab_ref, grid_ref, share_ref,
    own, to_up, to_down, from_down, from_up, base, lean_ref, inverse_h,
    field, sent, held, spread, gain, z_hi, z_lo, weight, wide, target_ref,
    in_sem, halo_send, halo_recv, turn_send, turn_recv, own_sem,
):
    bands = lax.axis_size("lat")
    band = lax.axis_index("lat")
    group = lax.axis_index("lev")
    above = (lax.rem(band + 1, bands), group)
    below = (lax.rem(band + bands - 1, bands), group)
    partners = [(band, lax.rem(group + step, GROUPS)) for step in range(1, GROUPS)]

    has_below, has_above = band > 0, band < bands - 1
    barrier = pltpu.get_barrier_semaphore()

    def greet(device):
        pl.semaphore_signal(barrier, inc=1, device_id=device, device_id_type=MESH)

    for device in partners:
        greet(device)
    pl.when(has_below)(lambda: greet(below))
    pl.when(has_above)(lambda: greet(above))

    loads = [
        pltpu.make_async_copy(source, given.at[item], in_sem.at[item])
        for item, source in enumerate((h_hbm, v_hbm, u_hbm, t_hbm))
    ]
    tables = [
        pltpu.make_async_copy(grid_hbm.at[band], grid_ref, in_sem.at[4]),
        pltpu.make_async_copy(tab_hbm, tab_ref, in_sem.at[5]),
        pltpu.make_async_copy(share_hbm, share_ref, in_sem.at[6]),
        pltpu.make_async_copy(mat_hbm, mat_ref, in_sem.at[7]),
    ]
    for copy in loads + tables:
        copy.start()

    @pl.when(jnp.logical_not(has_below))
    def _():
        from_down[...] = jnp.zeros_like(from_down)

    @pl.when(jnp.logical_not(has_above))
    def _():
        from_up[...] = jnp.zeros_like(from_up)

    def sub_row(shape):
        return lax.rem(lax.broadcasted_iota(jnp.int32, shape, 0), ROWS)

    place = sub_row((8, WIDE))

    def down(array, step):
        return pltpu.roll(array, step % 8, 0)

    def side(array, step):
        return pltpu.roll(array, step % WIDE, 1)

    def cut_item(item):
        for pair in range(2):

            def load(first, last):
                value = given[item, 2 * pair : 2 * pair + 2, :, first : min(last, LON)]
                value = value.reshape(8, min(last, LON) - first)
                short = -value.shape[1] % 128
                if short:
                    value = jnp.concatenate([value, jnp.zeros((8, short), jnp.float32)], axis=1)
                return value

            for block in range(COARSE):
                own[item, block, pair] = window(load, block)

        def edges(block, carry):
            a, b = own[item, block, 0], own[item, block, 1]
            to_up[item, block] = jnp.where(
                place < 2,
                jnp.where(place == 0, down(a, -3), down(b, -2)),
                jnp.where(place == 2, a, down(b, 1)),
            )
            to_down[item, block] = jnp.where(
                place < 2,
                jnp.where(place == 0, down(b, -1), a),
                jnp.where(place == 2, down(b, 2), down(a, 3)),
            )
            return carry

        lax.fori_loop(0, COARSE, edges, 0)

    def halo(item, way):
        return pltpu.make_async_remote_copy(
            src_ref=(to_down if way else to_up).at[item],
            dst_ref=(from_up if way else from_down).at[item],
            send_sem=halo_send.at[item, way],
            recv_sem=halo_recv.at[item, way],
            device_id=below if way else above,
            device_id_type=MESH,
        )

    def start_halo(item):
        pl.when(has_above)(lambda: halo(item, 0).start())
        pl.when(has_below)(lambda: halo(item, 1).start())

    def drain_halo(item):
        pl.when(has_above)(lambda: halo(item, 0).wait_send())
        pl.when(has_below)(lambda: halo(item, 1).wait_send())

    for item in range(4):
        loads[item].wait()
        cut_item(item)
        if item == 0:
            pl.semaphore_wait(
                barrier,
                len(partners) + jnp.where(has_below, 1, 0) + jnp.where(has_above, 1, 0),
            )
        if item < 2:
            start_halo(item)
    for copy in tables:
        copy.wait()

    def zonal(block, carry):
        for pair in range(2):
            wind = own[2, block, pair]
            thick = own[0, block, pair]
            c = SPEED * (wind + side(wind, -1))
            up = c >= 0.0
            part = limits(c)
            for item in range(4):
                q = thick if item == 0 else thick * own[item, block, pair]
                before, after, later = side(q, 1), side(q, -1), side(q, -2)
                step = after - q
                first = jnp.where(up, q - before, later - after)
                through = c * (jnp.where(up, q, after) + part * minmod(first, step))
                base[item, block, pair] = q - (through - side(through, 1))
        return carry

    lax.fori_loop(0, COARSE, zonal, 0, unroll=2)

    ratio = jnp.concatenate([grid_ref[3], grid_ref[3]], axis=1)
    for order in range(WAVES):
        sine = jnp.broadcast_to(tab_ref[2, order : order + 1, :], (8, WIDE))
        damping = ratio / jnp.maximum(sine, ratio)
        damping = damping * damping * ((1.0 if order in (0, 6) else 2.0) / LON)
        gain[16 * order : 16 * order + 8] = damping
        gain[16 * order + 8 : 16 * order + 16] = damping


    def outer(a, b):
        return jnp.where(
            place == 1, down(b, 1), jnp.where(place == 2, down(b, -1), a)
        )

    def wide_grid(index):
        return jnp.concatenate([grid_ref[index], grid_ref[index]], axis=1)

    def slants(block, carry):
        a, b = own[1, block, 0], own[1, block, 1]
        near = jnp.where(place < 2, from_down[1, block], from_up[1, block])
        winds = (a + down(a, -1), b + down(b, -1), near + outer(a, b))
        for index, wind in enumerate(winds):
            c = SPEED * wind
            lean_ref[block, 2 * index] = c * wide_grid(2 if index == 2 else 1)
            lean_ref[block, 2 * index + 1] = limits(c)
        return carry

    def meridional(item):
        def one(block, carry):
            sign = jnp.where(place < 2, 1.0, -1.0)
            low, high = from_down[0, block], from_up[0, block]
            cells = [own[0, block, 0], own[0, block, 1]]
            if item:
                low, high = low * from_down[item, block], high * from_up[item, block]
                cells = [cells[pair] * own[item, block, pair] for pair in range(2)]
            near = jnp.where(place < 2, low, high)
            far = jnp.where(place < 2, down(low, -2), down(high, 2))
            edge = outer(*cells)
            gap = edge - near
            near_slope = sign * minmod(near - far, gap)
            gap = sign * gap
            slopes, flows = [], []
            for pair in range(2):
                x = cells[pair]
                after = down(x, -1)
                inner = after - x
                upper = jnp.where(place == 3, down(gap, 1) if pair else gap, inner)
                lower = jnp.where(place == 0, down(gap, -1) if pair else gap, down(inner, 1))
                slope = minmod(lower, upper)
                slopes.append(slope)
                part = lean_ref[block, 2 * pair + 1]
                up = part > 0.0
                flows.append(
                    lean_ref[block, 2 * pair]
                    * (jnp.where(up, x, after) + part * jnp.where(up, slope, down(slope, -1)))
                )
            part = lean_ref[block, 5]
            pick = part * sign > 0.0
            flow = lean_ref[block, 4] * (
                jnp.where(pick, near, edge) + part * jnp.where(pick, near_slope, outer(*slopes))
            )
            for pair in range(2):
                above_flow = jnp.where(place == 3, down(flow, 1) if pair else flow, flows[pair])
                below_flow = jnp.where(
                    place == 0, down(flow, -1) if pair else flow, down(flows[pair], 1)
                )
                value = base[item, block, pair] - (above_flow - below_flow) * wide_grid(0)
                rows = pl.ds(8 * pair, 8)
                if item == 0:
                    sent[0, block, rows] = value
                    inverse_h[block, rows] = 1.0 / value
                else:
                    field[block, rows] = value * inverse_h[block, rows]
            return carry

        lax.fori_loop(0, COARSE, one, 0, unroll=2)

    def turn(item, step):
        target = lax.rem(group + step, GROUPS)
        return pltpu.make_async_remote_copy(
            src_ref=sent.at[item, pl.ds(PER * target, PER)],
            dst_ref=held.at[item, group],
            send_sem=turn_send.at[item, step - 1],
            recv_sem=turn_recv.at[item, step - 1],
            device_id=(band, target),
            device_id_type=MESH,
        )

    def keep(item):
        return pltpu.make_async_copy(
            sent.at[item, pl.ds(PER * group, PER)], held.at[item, group], own_sem.at[item]
        )

    def start_turn(item):
        for step in (2, 3, 1):
            turn(item, step).start()
        keep(item).start()

    def end_turn(item):
        for step in range(1, GROUPS):
            source = lax.rem(group + GROUPS - step, GROUPS)
            pltpu.make_async_remote_copy(
                src_ref=sent.at[item, pl.ds(0, PER)],
                dst_ref=held.at[item, source],
                send_sem=turn_send.at[item, step - 1],
                recv_sem=turn_recv.at[item, step - 1],
                device_id=(band, source),
                device_id_type=MESH,
            ).wait_recv()
        keep(item).wait()

    def product(index):
        high, low = z_hi[...], z_lo[...]
        return (
            jnp.dot(high, mat_ref[index], preferred_element_type=jnp.float32)
            + jnp.dot(low, mat_ref[index], preferred_element_type=jnp.float32)
            + jnp.dot(high, mat_ref[index + 1], preferred_element_type=jnp.float32)
        )

    def polar(item):
        def forward(tile, carry):
            lanes = pl.ds(pl.multiple_of(128 * tile, 128), 128)
            real, imag = forward_blocks([field[block, :, lanes] for block in range(COARSE)])
            for order in range(WAVES):
                cos = jnp.broadcast_to(tab_ref[0, order : order + 1, lanes], (16, 128))
                sin = jnp.broadcast_to(tab_ref[1, order : order + 1, lanes], (16, 128))
                if imag[order] is None:
                    parts = (real[order] * cos, -(real[order] * sin))
                else:
                    parts = (
                        real[order] * cos + imag[order] * sin,
                        imag[order] * cos - real[order] * sin,
                    )
                for half, part in enumerate(parts):
                    at = pl.multiple_of(WIDE * half + 128 * tile, 128)
                    spot = (pl.ds(16 * order, 16), pl.ds(at, 128))
                    high = part.astype(jnp.bfloat16)
                    z_hi[spot] = high
                    z_lo[spot] = (part - high.astype(jnp.float32)).astype(jnp.bfloat16)
            return carry

        lax.fori_loop(0, 2, forward, 0, unroll=True)
        damping = gain[...]
        waves = product(0) * jnp.concatenate([damping, damping], axis=1)
        high = waves.astype(jnp.bfloat16)
        z_hi[...] = high
        z_lo[...] = (waves - high.astype(jnp.float32)).astype(jnp.bfloat16)
        spread[...] = product(2)

        def backward(tile, carry):
            lanes = pl.ds(pl.multiple_of(128 * tile, 128), 128)
            other = pl.ds(pl.multiple_of(WIDE + 128 * tile, 128), 128)
            real, imag = [], []
            for order in range(WAVES):
                rows = pl.ds(16 * order, 16)
                cos = jnp.broadcast_to(tab_ref[0, order : order + 1, lanes], (16, 128))
                sin = jnp.broadcast_to(tab_ref[1, order : order + 1, lanes], (16, 128))
                re, im = spread[rows, lanes], spread[rows, other]
                real.append(re * cos - im * sin)
                imag.append(im * cos + re * sin)
            for block, value in enumerate(backward_blocks(real, imag)):
                sent[item, block, :, lanes] = value
            return carry

        lax.fori_loop(0, 2, backward, 0, unroll=True)

    def end_halo(item):
        pl.when(has_below)(lambda: halo(item, 0).wait_recv())
        pl.when(has_above)(lambda: halo(item, 1).wait_recv())

    drain_halo(0)
    drain_halo(1)
    start_halo(2)
    end_halo(0)
    end_halo(1)
    lax.fori_loop(0, COARSE, slants, 0)
    meridional(0)
    start_turn(0)
    for item in range(1, 4):
        if item > 1:
            end_halo(item)
        meridional(item)
        if item == 1:
            drain_halo(2)
            start_halo(3)
        polar(item)
        start_turn(item)
    drain_halo(3)

    first_half = lax.broadcasted_iota(jnp.int32, (8, 128), 0) < ROWS

    def lines(item, block, lanes):
        found = []
        for index in range(8):
            both = held[item, index // 2, block, pl.ds(8 * (index % 2), 8), lanes]
            turned = down(both, ROWS)
            found.append(jnp.where(first_half, both, turned))
            found.append(jnp.where(first_half, turned, both))
        return found

    def tile_of(step):
        return step // 2, pl.ds(pl.multiple_of(128 * lax.rem(step, 2), 128), 128)

    def weigh(step, carry):
        uppers = []
        for line in lines(0, *tile_of(step)):
            uppers.append(uppers[-1] + line if uppers else line)
        total = uppers[-1]
        lowers = [jnp.zeros((8, 128), jnp.float32)] + uppers[:-1]
        running = share_ref[0]
        for level in range(1, 16):
            running = running + share_ref[level]
        unit = total / jnp.full((8, 128), running)
        running = jnp.float32(0.0)
        for pair in range(8):
            one, two = share_ref[2 * pair], share_ref[2 * pair + 1]
            target = unit * jnp.where(first_half, one, two)
            top = unit * jnp.where(first_half, running + one, running + one + two)
            running = running + one + two
            bottom = top - target
            wide[pair, step] = target
            target_ref[step, pair] = 1.0 / target
            for index in range(16):
                weight[step, pair, index] = jnp.maximum(
                    jnp.minimum(top, uppers[index]) - jnp.maximum(bottom, lowers[index]), 0.0
                )
        return carry

    def gather(item):
        def one(step, carry):
            found = lines(item, *tile_of(step))
            for pair in range(8):
                total = weight[step, pair, 0] * found[0]
                for index in range(1, 16):
                    total = total + weight[step, pair, index] * found[index]
                wide[pair, step] = total * target_ref[step, pair]
            return carry

        lax.fori_loop(0, 2 * PER, one, 0, unroll=2)

    def pack(output):
        def one(pair, carry):
            lane = lax.broadcasted_iota(jnp.int32, (8, 128), 1)
            shifts = (128 - EDGE, 104, 88)
            t = [pltpu.roll(wide[pair, step], shifts[step // 2], 1) for step in range(6)]
            tiles = [
                jnp.where(lane < 120, t[0], t[1]),
                jnp.where(lane < 112, t[1], t[2]),
                jnp.where(lane < 104, t[2], t[3]),
                jnp.where(lane < 96, t[3], t[4]),
                jnp.where(lane < 88, t[4], t[5]),
                t[5],
            ]
            for at, tile in enumerate(tiles):
                size = min(128, LON // GROUPS - 128 * at)
                value = tile[:, :size].reshape(2, ROWS, size)
                out_ref[output, pl.ds(2 * pair, 2), :, 128 * at : 128 * at + size] = value
            return carry

        lax.fori_loop(0, 8, one, 0, unroll=True)

    end_turn(0)
    lax.fori_loop(0, 2 * PER, weigh, 0)
    pack(3)
    for item in range(1, 4):
        end_turn(item)
        gather(item)
        pack((0, 2, 1, 0)[item])

    for item in range(4):
        for step in range(1, GROUPS):
            turn(item, step).wait_send()


def on_device(
    zonal_velocity, meridional_velocity, heat_anomaly, layer_pressure_depth, reference_layer_shares
):
    matrices, tables = constants()
    f32 = jnp.float32
    hbm = pl.BlockSpec(memory_space=pltpu.HBM)
    size = 16 * WAVES
    operands = (
        jnp.asarray(grid_table(lax.axis_size("lat"))),
        reference_layer_shares,
        zonal_velocity,
        meridional_velocity,
        heat_anomaly,
        layer_pressure_depth,
        jnp.asarray(matrices),
        jnp.asarray(tables),
    )
    result = pl.pallas_call(
        kernel,
        out_shape=jax.ShapeDtypeStruct((4, 16, ROWS, LON // GROUPS), f32),
        in_specs=[hbm] * 8,
        out_specs=pl.BlockSpec(memory_space=pltpu.VMEM),
        scratch_shapes=[
            pltpu.VMEM((4, LEVELS, ROWS, LON), f32),
            pltpu.VMEM((4, 2 * WIDE, 2 * WIDE), jnp.bfloat16),
            pltpu.VMEM((3, 8, WIDE), f32),
            pltpu.VMEM((4, 8, 128), f32),
            pltpu.SMEM((16,), f32),
            pltpu.VMEM((4, COARSE, 2, 8, WIDE), f32),
            pltpu.VMEM((4, COARSE, 8, WIDE), f32),
            pltpu.VMEM((4, COARSE, 8, WIDE), f32),
            pltpu.VMEM((4, COARSE, 8, WIDE), f32),
            pltpu.VMEM((4, COARSE, 8, WIDE), f32),
            pltpu.VMEM((4, COARSE, 2, 8, WIDE), f32),
            pltpu.VMEM((COARSE, 6, 8, WIDE), f32),
            pltpu.VMEM((COARSE, 16, WIDE), f32),
            pltpu.VMEM((COARSE, 16, WIDE), f32),
            pltpu.VMEM((4, COARSE, 16, WIDE), f32),
            pltpu.VMEM((4, GROUPS, PER, 16, WIDE), f32),
            pltpu.VMEM((size, 2 * WIDE), f32),
            pltpu.VMEM((size, WIDE), f32),
            pltpu.VMEM((size, 2 * WIDE), jnp.bfloat16),
            pltpu.VMEM((size, 2 * WIDE), jnp.bfloat16),
            pltpu.VMEM((2 * PER, 8, 16, 8, 128), f32),
            pltpu.VMEM((8, 2 * PER, 8, 128), f32),
            pltpu.VMEM((2 * PER, 8, 8, 128), f32),
            pltpu.SemaphoreType.DMA((8,)),
            pltpu.SemaphoreType.DMA((4, 2)),
            pltpu.SemaphoreType.DMA((4, 2)),
            pltpu.SemaphoreType.DMA((4, 3)),
            pltpu.SemaphoreType.DMA((4, 3)),
            pltpu.SemaphoreType.DMA((4,)),
        ],
        compiler_params=pltpu.CompilerParams(
            collective_id=0, has_side_effects=True, vmem_limit_bytes=24 << 20
        ),
        cost_estimate=pl.CostEstimate(
            flops=2_000_000_000, bytes_accessed=4_000_000, transcendentals=0
        ),
    )(*(pltpu.with_memory_space_constraint(array, pltpu.HBM) for array in operands))
    return (result[0], result[1], result[2], result[3])


def solution(mesh):
    return jax.shard_map(
        on_device,
        mesh=mesh,
        in_specs=(
            P("lev", "lat", None),
            P("lev", "lat", None),
            P("lev", "lat", None),
            P("lev", "lat", None),
            P(),
        ),
        out_specs=(
            P(None, "lat", "lev"),
            P(None, "lat", "lev"),
            P(None, "lat", "lev"),
            P(None, "lat", "lev"),
        ),
        check_vma=False,
    )
```

```python
import math

import jax
import jax.numpy as jnp
import numpy as np
from jax import lax
from jax.experimental import pallas as pl
from jax.experimental.pallas import tpu as pltpu
from jax.sharding import PartitionSpec as P

SPEED = 0.04
QUARTER = math.cos(math.pi / 4.0)
SPACING = 180.0 / 1440.0
LON = 2880
ROWS = 4
LEVELS = 4
GROUPS = 4
COARSE = 12
FINE = 240
WIDE = 256
EDGE = 8
PER = COARSE // GROUPS
WAVES = COARSE // 2 + 1
ORDER = (2, 3, 1, 0)
MESH = pl.DeviceIdType.MESH


def grid_table(bands):
    f32 = np.float32
    rows = np.arange(bands * ROWS)
    faces = np.arange(bands * ROWS + 1)
    scale = f32(math.pi / 180.0)
    center = np.cos(((rows.astype(f32) + f32(0.5)) * f32(SPACING) - f32(90.0)) * scale)
    face = np.cos((faces.astype(f32) * f32(SPACING) - f32(90.0)) * scale)
    face = np.where(faces == 0, f32(0.0), face)
    table = np.zeros((bands, 4, 8, 128), f32)
    for sub in range(8):
        row = ROWS * np.arange(bands) + sub % ROWS
        table[:, 0, sub] = (f32(1.0) / center[row])[:, None]
        table[:, 1, sub] = face[row + 1][:, None]
        outer = ROWS * np.arange(bands) + (0 if sub % ROWS < 2 else ROWS)
        table[:, 2, sub] = face[outer][:, None]
        table[:, 3, sub] = (center[row] / f32(QUARTER))[:, None]
    return table


def split_bf16(array):
    high = array.astype(jnp.bfloat16)
    low = (array - high.astype(np.float32)).astype(jnp.bfloat16)
    return high, low


def constants():
    cell = np.arange(FINE)
    wave = np.arange(FINE)
    angle = 2.0 * np.pi * (np.outer(cell, wave) % FINE) / FINE
    cos, sin = np.cos(angle), np.sin(angle)
    forward = np.zeros((2 * WIDE, 2 * WIDE))
    spots = slice(EDGE, EDGE + FINE)
    spots_im = slice(WIDE + EDGE, WIDE + EDGE + FINE)
    forward[spots, 0:FINE] = cos
    forward[spots, WIDE : WIDE + FINE] = -sin
    forward[spots_im, 0:FINE] = sin
    forward[spots_im, WIDE : WIDE + FINE] = cos
    backward = np.zeros((2 * WIDE, 2 * WIDE))
    backward[0:FINE, spots] = cos.T
    backward[0:FINE, spots_im] = sin.T
    backward[WIDE : WIDE + FINE, spots] = -sin.T
    backward[WIDE : WIDE + FINE, spots_im] = cos.T
    matrices = np.stack(
        [m for whole in (forward, backward) for m in split_bf16(whole.astype(np.float32))]
    )
    tables = np.zeros((3, 8, WIDE), np.float32)
    for order in range(WAVES):
        turn = 2.0 * np.pi * order * cell / LON
        tables[0, order, spots] = np.cos(turn)
        tables[1, order, spots] = np.sin(turn)
        number = (order + COARSE * wave).astype(np.float32)
        tables[2, order, 0:FINE] = np.sin(number * np.float32(math.pi / LON))
    return matrices, tables


def cos_of(index):
    value = math.cos(2.0 * math.pi * index / COARSE)
    return round(value) if abs(value - round(value)) < 1e-9 else round(2 * value) / 2 if abs(
        2 * value - round(2 * value)
    ) < 1e-9 else value


def combine(terms):
    total = None
    for factor, array in terms:
        if factor == 0:
            continue
        if total is None:
            total = array if factor == 1 else -array if factor == -1 else factor * array
        elif factor == 1:
            total = total + array
        elif factor == -1:
            total = total - array
        else:
            total = total + factor * array
    return total


def forward_blocks(x):
    even = {n: x[n] + x[COARSE - n] for n in range(1, 6)}
    odd = {n: x[n] - x[COARSE - n] for n in range(1, 6)}
    ends = {0: x[0] + x[6], 1: x[0] - x[6]}
    even_sum = {n: even[n] + even[6 - n] for n in (1, 2)}
    even_dif = {n: even[n] - even[6 - n] for n in (1, 2)}
    odd_sum = {n: odd[n] + odd[6 - n] for n in (1, 2)}
    odd_dif = {n: odd[n] - odd[6 - n] for n in (1, 2)}
    real, imag = [], []
    for k in range(WAVES):
        pick = even_dif if k % 2 else even_sum
        terms = [(1, ends[k % 2])] + [(cos_of(n * k), pick[n]) for n in (1, 2)]
        terms.append((cos_of(3 * k), even[3]))
        real.append(combine(terms))
        if 0 < k < 6:
            pick = odd_sum if k % 2 else odd_dif
            terms = [(-cos_of(n * k - 3), pick[n]) for n in (1, 2)]
            terms.append((-cos_of(3 * k - 3), odd[3]))
            imag.append(combine(terms))
        else:
            imag.append(None)
    return real, imag


def backward_blocks(real, imag):
    base = {0: real[0] + real[6], 1: real[0] - real[6]}
    blocks = [None] * COARSE
    for b in range(0, 7):
        cosine = combine([(1, base[b % 2])] + [(cos_of(k * b), real[k]) for k in range(1, 6)])
        if b in (0, 6):
            blocks[b] = cosine
            continue
        sine = combine([(-cos_of(k * b - 3), imag[k]) for k in range(1, 6)])
        blocks[b] = cosine + sine
        blocks[COARSE - b] = cosine - sine
    return blocks


def minmod(left, right):
    return jnp.maximum(jnp.minimum(left, right), 0.0) + jnp.minimum(jnp.maximum(left, right), 0.0)


def window(load, block):
    lane = lax.broadcasted_iota(jnp.int32, (8, WIDE), 1)
    if block == 0:
        body = pltpu.roll(load(0, 256), EDGE, 1)
        tail = pltpu.roll(load(2816, LON), 128 - (LON - EDGE - 2816), 1)
        return jnp.concatenate(
            [jnp.where(lane[:, :128] < EDGE, tail, body[:, :128]), body[:, 128:]], axis=1
        )
    start = FINE * block - EDGE
    first = start // 128 * 128
    body = pltpu.roll(load(first, first + 384), (384 - (start - first)) % 384, 1)[:, :WIDE]
    if block == COARSE - 1:
        head = pltpu.roll(load(0, 256), WIDE - EDGE, 1)
        body = jnp.where(lane >= WIDE - EDGE, head, body)
    return body


def limits(courant):
    return jnp.where(courant >= 0.0, 0.5, -0.5) - 0.5 * courant


def kernel(
    grid_hbm, share_hbm, u_hbm, v_hbm, t_hbm, h_hbm, mat_hbm, tab_hbm,
    out_ref,
    given, mat_ref, tab_ref, grid_ref, share_ref,
    own, to_up, to_down, from_down, from_up, base, lean_ref, inverse_h,
    field, sent, held, spread, gain, z_hi, z_lo, weight, wide, target_ref,
    in_sem, halo_send, halo_recv, turn_send, turn_recv, own_sem,
):
    bands = lax.axis_size("lat")
    band = lax.axis_index("lat")
    group = lax.axis_index("lev")
    above = (lax.rem(band + 1, bands), group)
    below = (lax.rem(band + bands - 1, bands), group)
    partners = [(band, lax.rem(group + step, GROUPS)) for step in range(1, GROUPS)]

    has_below, has_above = band > 0, band < bands - 1
    barrier = pltpu.get_barrier_semaphore()

    def greet(device):
        pl.semaphore_signal(barrier, inc=1, device_id=device, device_id_type=MESH)

    for device in partners:
        greet(device)
    pl.when(has_below)(lambda: greet(below))
    pl.when(has_above)(lambda: greet(above))

    loads = [
        pltpu.make_async_copy(source, given.at[item], in_sem.at[item])
        for item, source in enumerate((h_hbm, v_hbm, u_hbm, t_hbm))
    ]
    tables = [
        pltpu.make_async_copy(grid_hbm.at[band], grid_ref, in_sem.at[4]),
        pltpu.make_async_copy(tab_hbm, tab_ref, in_sem.at[5]),
        pltpu.make_async_copy(share_hbm, share_ref, in_sem.at[6]),
        pltpu.make_async_copy(mat_hbm, mat_ref, in_sem.at[7]),
    ]
    for copy in loads + tables:
        copy.start()

    @pl.when(jnp.logical_not(has_below))
    def _():
        from_down[...] = jnp.zeros_like(from_down)

    @pl.when(jnp.logical_not(has_above))
    def _():
        from_up[...] = jnp.zeros_like(from_up)

    def sub_row(shape):
        return lax.rem(lax.broadcasted_iota(jnp.int32, shape, 0), ROWS)

    place = sub_row((8, WIDE))

    def down(array, step):
        return pltpu.roll(array, step % 8, 0)

    def side(array, step):
        return pltpu.roll(array, step % WIDE, 1)

    def cut_item(item):
        for pair in range(2):

            def load(first, last):
                value = given[item, 2 * pair : 2 * pair + 2, :, first : min(last, LON)]
                value = value.reshape(8, min(last, LON) - first)
                short = -value.shape[1] % 128
                if short:
                    value = jnp.concatenate([value, jnp.zeros((8, short), jnp.float32)], axis=1)
                return value

            for block in range(COARSE):
                own[item, block, pair] = window(load, block)

        def edges(block, carry):
            a, b = own[item, block, 0], own[item, block, 1]
            to_up[item, block] = jnp.where(
                place < 2,
                jnp.where(place == 0, down(a, -3), down(b, -2)),
                jnp.where(place == 2, a, down(b, 1)),
            )
            to_down[item, block] = jnp.where(
                place < 2,
                jnp.where(place == 0, down(b, -1), a),
                jnp.where(place == 2, down(b, 2), down(a, 3)),
            )
            return carry

        lax.fori_loop(0, COARSE, edges, 0)

    def home(step):
        return PER * lax.rem(group + step, GROUPS)

    def halo(item, way, step):
        spot = (item, pl.ds(home(step), PER)) if item < 2 else (item,)
        return pltpu.make_async_remote_copy(
            src_ref=(to_down if way else to_up).at[spot],
            dst_ref=(from_up if way else from_down).at[spot],
            send_sem=halo_send.at[item, way, step],
            recv_sem=halo_recv.at[item, way, step],
            device_id=below if way else above,
            device_id_type=MESH,
        )

    def start_halo(item, step=0):
        pl.when(has_above)(lambda: halo(item, 0, step).start())
        pl.when(has_below)(lambda: halo(item, 1, step).start())

    def drain_halo(item, step=0):
        pl.when(has_above)(lambda: halo(item, 0, step).wait_send())
        pl.when(has_below)(lambda: halo(item, 1, step).wait_send())

    for item in range(4):
        loads[item].wait()
        cut_item(item)
        if item == 0:
            pl.semaphore_wait(
                barrier,
                len(partners) + jnp.where(has_below, 1, 0) + jnp.where(has_above, 1, 0),
            )
        if item == 1:
            for step in ORDER:
                start_halo(0, step)
                start_halo(1, step)
        elif item == 2:
            start_halo(2)
    for copy in tables:
        copy.wait()

    def zonal(block, carry):
        for pair in range(2):
            wind = own[2, block, pair]
            thick = own[0, block, pair]
            c = SPEED * (wind + side(wind, -1))
            up = c >= 0.0
            part = limits(c)
            for item in range(4):
                q = thick if item == 0 else thick * own[item, block, pair]
                before, after, later = side(q, 1), side(q, -1), side(q, -2)
                step = after - q
                first = jnp.where(up, q - before, later - after)
                through = c * (jnp.where(up, q, after) + part * minmod(first, step))
                base[item, block, pair] = q - (through - side(through, 1))
        return carry

    lax.fori_loop(0, COARSE, zonal, 0, unroll=2)

    start_halo(3)
    ratio = jnp.concatenate([grid_ref[3], grid_ref[3]], axis=1)
    for order in range(WAVES):
        sine = jnp.broadcast_to(tab_ref[2, order : order + 1, :], (8, WIDE))
        damping = ratio / jnp.maximum(sine, ratio)
        damping = damping * damping * ((1.0 if order in (0, 6) else 2.0) / LON)
        gain[16 * order : 16 * order + 8] = damping
        gain[16 * order + 8 : 16 * order + 16] = damping


    def outer(a, b):
        return jnp.where(
            place == 1, down(b, 1), jnp.where(place == 2, down(b, -1), a)
        )

    def wide_grid(index):
        return jnp.concatenate([grid_ref[index], grid_ref[index]], axis=1)

    def slants(block, carry):
        a, b = own[1, block, 0], own[1, block, 1]
        near = jnp.where(place < 2, from_down[1, block], from_up[1, block])
        winds = (a + down(a, -1), b + down(b, -1), near + outer(a, b))
        for index, wind in enumerate(winds):
            c = SPEED * wind
            lean_ref[block, 2 * index] = c * wide_grid(2 if index == 2 else 1)
            lean_ref[block, 2 * index + 1] = limits(c)
        return carry

    def meridional(item, step=None):
        def one(block, carry):
            if step is not None:
                block = home(step) + block
                slants(block, carry)
            sign = jnp.where(place < 2, 1.0, -1.0)
            low, high = from_down[0, block], from_up[0, block]
            cells = [own[0, block, 0], own[0, block, 1]]
            if item:
                low, high = low * from_down[item, block], high * from_up[item, block]
                cells = [cells[pair] * own[item, block, pair] for pair in range(2)]
            near = jnp.where(place < 2, low, high)
            far = jnp.where(place < 2, down(low, -2), down(high, 2))
            edge = outer(*cells)
            gap = edge - near
            near_slope = sign * minmod(near - far, gap)
            gap = sign * gap
            slopes, flows = [], []
            for pair in range(2):
                x = cells[pair]
                after = down(x, -1)
                inner = after - x
                upper = jnp.where(place == 3, down(gap, 1) if pair else gap, inner)
                lower = jnp.where(place == 0, down(gap, -1) if pair else gap, down(inner, 1))
                slope = minmod(lower, upper)
                slopes.append(slope)
                part = lean_ref[block, 2 * pair + 1]
                up = part > 0.0
                flows.append(
                    lean_ref[block, 2 * pair]
                    * (jnp.where(up, x, after) + part * jnp.where(up, slope, down(slope, -1)))
                )
            part = lean_ref[block, 5]
            pick = part * sign > 0.0
            flow = lean_ref[block, 4] * (
                jnp.where(pick, near, edge) + part * jnp.where(pick, near_slope, outer(*slopes))
            )
            for pair in range(2):
                above_flow = jnp.where(place == 3, down(flow, 1) if pair else flow, flows[pair])
                below_flow = jnp.where(
                    place == 0, down(flow, -1) if pair else flow, down(flows[pair], 1)
                )
                value = base[item, block, pair] - (above_flow - below_flow) * wide_grid(0)
                rows = pl.ds(8 * pair, 8)
                if item == 0:
                    sent[0, block, rows] = value
                    inverse_h[block, rows] = 1.0 / value
                else:
                    field[block, rows] = value * inverse_h[block, rows]
            return carry

        if step is None:
            lax.fori_loop(0, COARSE, one, 0, unroll=2)
        else:
            lax.fori_loop(0, PER, one, 0, unroll=True)

    def turn(item, step):
        target = lax.rem(group + step, GROUPS)
        return pltpu.make_async_remote_copy(
            src_ref=sent.at[item, pl.ds(PER * target, PER)],
            dst_ref=held.at[item, group],
            send_sem=turn_send.at[item, step - 1],
            recv_sem=turn_recv.at[item, step - 1],
            device_id=(band, target),
            device_id_type=MESH,
        )

    def keep(item):
        return pltpu.make_async_copy(
            sent.at[item, pl.ds(PER * group, PER)], held.at[item, group], own_sem.at[item]
        )

    def start_turn(item):
        for step in (2, 3, 1):
            turn(item, step).start()
        keep(item).start()

    def end_turn(item):
        for step in range(1, GROUPS):
            source = lax.rem(group + GROUPS - step, GROUPS)
            pltpu.make_async_remote_copy(
                src_ref=sent.at[item, pl.ds(0, PER)],
                dst_ref=held.at[item, source],
                send_sem=turn_send.at[item, step - 1],
                recv_sem=turn_recv.at[item, step - 1],
                device_id=(band, source),
                device_id_type=MESH,
            ).wait_recv()
        keep(item).wait()

    def product(index):
        high, low = z_hi[...], z_lo[...]
        return (
            jnp.dot(high, mat_ref[index], preferred_element_type=jnp.float32)
            + jnp.dot(low, mat_ref[index], preferred_element_type=jnp.float32)
            + jnp.dot(high, mat_ref[index + 1], preferred_element_type=jnp.float32)
        )

    def polar(item):
        def forward(tile, carry):
            lanes = pl.ds(pl.multiple_of(128 * tile, 128), 128)
            real, imag = forward_blocks([field[block, :, lanes] for block in range(COARSE)])
            for order in range(WAVES):
                cos = jnp.broadcast_to(tab_ref[0, order : order + 1, lanes], (16, 128))
                sin = jnp.broadcast_to(tab_ref[1, order : order + 1, lanes], (16, 128))
                if imag[order] is None:
                    parts = (real[order] * cos, -(real[order] * sin))
                else:
                    parts = (
                        real[order] * cos + imag[order] * sin,
                        imag[order] * cos - real[order] * sin,
                    )
                for half, part in enumerate(parts):
                    at = pl.multiple_of(WIDE * half + 128 * tile, 128)
                    spot = (pl.ds(16 * order, 16), pl.ds(at, 128))
                    high = part.astype(jnp.bfloat16)
                    z_hi[spot] = high
                    z_lo[spot] = (part - high.astype(jnp.float32)).astype(jnp.bfloat16)
            return carry

        lax.fori_loop(0, 2, forward, 0, unroll=True)
        damping = gain[...]
        waves = product(0) * jnp.concatenate([damping, damping], axis=1)
        high = waves.astype(jnp.bfloat16)
        z_hi[...] = high
        z_lo[...] = (waves - high.astype(jnp.float32)).astype(jnp.bfloat16)
        spread[...] = product(2)

        def backward(tile, carry):
            lanes = pl.ds(pl.multiple_of(128 * tile, 128), 128)
            other = pl.ds(pl.multiple_of(WIDE + 128 * tile, 128), 128)
            real, imag = [], []
            for order in range(WAVES):
                rows = pl.ds(16 * order, 16)
                cos = jnp.broadcast_to(tab_ref[0, order : order + 1, lanes], (16, 128))
                sin = jnp.broadcast_to(tab_ref[1, order : order + 1, lanes], (16, 128))
                re, im = spread[rows, lanes], spread[rows, other]
                real.append(re * cos - im * sin)
                imag.append(im * cos + re * sin)
            for block, value in enumerate(backward_blocks(real, imag)):
                sent[item, block, :, lanes] = value
            return carry

        lax.fori_loop(0, 2, backward, 0, unroll=True)

    def end_halo(item, step=0):
        pl.when(has_below)(lambda: halo(item, 0, step).wait_recv())
        pl.when(has_above)(lambda: halo(item, 1, step).wait_recv())

    for step in ORDER:
        end_halo(0, step)
        end_halo(1, step)
        meridional(0, step)
        if step:
            turn(0, step).start()
        else:
            keep(0).start()
    for item in range(1, 4):
        if item > 1:
            end_halo(item)
        meridional(item)
        polar(item)
        start_turn(item)
    for step in ORDER:
        drain_halo(0, step)
        drain_halo(1, step)
    drain_halo(2)
    drain_halo(3)

    first_half = lax.broadcasted_iota(jnp.int32, (8, 128), 0) < ROWS

    def lines(item, block, lanes):
        found = []
        for index in range(8):
            both = held[item, index // 2, block, pl.ds(8 * (index % 2), 8), lanes]
            turned = down(both, ROWS)
            found.append(jnp.where(first_half, both, turned))
            found.append(jnp.where(first_half, turned, both))
        return found

    def tile_of(step):
        return step // 2, pl.ds(pl.multiple_of(128 * lax.rem(step, 2), 128), 128)

    def weigh(step, carry):
        uppers = []
        for line in lines(0, *tile_of(step)):
            uppers.append(uppers[-1] + line if uppers else line)
        total = uppers[-1]
        lowers = [jnp.zeros((8, 128), jnp.float32)] + uppers[:-1]
        running = share_ref[0]
        for level in range(1, 16):
            running = running + share_ref[level]
        unit = total / jnp.full((8, 128), running)
        running = jnp.float32(0.0)
        for pair in range(8):
            one, two = share_ref[2 * pair], share_ref[2 * pair + 1]
            target = unit * jnp.where(first_half, one, two)
            top = unit * jnp.where(first_half, running + one, running + one + two)
            running = running + one + two
            bottom = top - target
            wide[pair, step] = target
            target_ref[step, pair] = 1.0 / target
            for index in range(16):
                weight[step, pair, index] = jnp.maximum(
                    jnp.minimum(top, uppers[index]) - jnp.maximum(bottom, lowers[index]), 0.0
                )
        return carry

    def gather(item):
        def one(step, carry):
            found = lines(item, *tile_of(step))
            for pair in range(8):
                total = weight[step, pair, 0] * found[0]
                for index in range(1, 16):
                    total = total + weight[step, pair, index] * found[index]
                wide[pair, step] = total * target_ref[step, pair]
            return carry

        lax.fori_loop(0, 2 * PER, one, 0, unroll=2)

    def pack(output):
        def one(pair, carry):
            lane = lax.broadcasted_iota(jnp.int32, (8, 128), 1)
            shifts = (128 - EDGE, 104, 88)
            t = [pltpu.roll(wide[pair, step], shifts[step // 2], 1) for step in range(6)]
            tiles = [
                jnp.where(lane < 120, t[0], t[1]),
                jnp.where(lane < 112, t[1], t[2]),
                jnp.where(lane < 104, t[2], t[3]),
                jnp.where(lane < 96, t[3], t[4]),
                jnp.where(lane < 88, t[4], t[5]),
                t[5],
            ]
            for at, tile in enumerate(tiles):
                size = min(128, LON // GROUPS - 128 * at)
                value = tile[:, :size].reshape(2, ROWS, size)
                out_ref[output, pl.ds(2 * pair, 2), :, 128 * at : 128 * at + size] = value
            return carry

        lax.fori_loop(0, 8, one, 0, unroll=True)

    end_turn(0)
    lax.fori_loop(0, 2 * PER, weigh, 0)
    pack(3)
    for item in range(1, 4):
        end_turn(item)
        gather(item)
        pack((0, 2, 1, 0)[item])

    for item in range(4):
        for step in range(1, GROUPS):
            turn(item, step).wait_send()


def on_device(
    zonal_velocity, meridional_velocity, heat_anomaly, layer_pressure_depth, reference_layer_shares
):
    matrices, tables = constants()
    f32 = jnp.float32
    hbm = pl.BlockSpec(memory_space=pltpu.HBM)
    size = 16 * WAVES
    operands = (
        jnp.asarray(grid_table(lax.axis_size("lat"))),
        reference_layer_shares,
        zonal_velocity,
        meridional_velocity,
        heat_anomaly,
        layer_pressure_depth,
        jnp.asarray(matrices),
        jnp.asarray(tables),
    )
    result = pl.pallas_call(
        kernel,
        out_shape=jax.ShapeDtypeStruct((4, 16, ROWS, LON // GROUPS), f32),
        in_specs=[hbm] * 8,
        out_specs=pl.BlockSpec(memory_space=pltpu.VMEM),
        scratch_shapes=[
            pltpu.VMEM((4, LEVELS, ROWS, LON), f32),
            pltpu.VMEM((4, 2 * WIDE, 2 * WIDE), jnp.bfloat16),
            pltpu.VMEM((3, 8, WIDE), f32),
            pltpu.VMEM((4, 8, 128), f32),
            pltpu.SMEM((16,), f32),
            pltpu.VMEM((4, COARSE, 2, 8, WIDE), f32),
            pltpu.VMEM((4, COARSE, 8, WIDE), f32),
            pltpu.VMEM((4, COARSE, 8, WIDE), f32),
            pltpu.VMEM((4, COARSE, 8, WIDE), f32),
            pltpu.VMEM((4, COARSE, 8, WIDE), f32),
            pltpu.VMEM((4, COARSE, 2, 8, WIDE), f32),
            pltpu.VMEM((COARSE, 6, 8, WIDE), f32),
            pltpu.VMEM((COARSE, 16, WIDE), f32),
            pltpu.VMEM((COARSE, 16, WIDE), f32),
            pltpu.VMEM((4, COARSE, 16, WIDE), f32),
            pltpu.VMEM((4, GROUPS, PER, 16, WIDE), f32),
            pltpu.VMEM((size, 2 * WIDE), f32),
            pltpu.VMEM((size, WIDE), f32),
            pltpu.VMEM((size, 2 * WIDE), jnp.bfloat16),
            pltpu.VMEM((size, 2 * WIDE), jnp.bfloat16),
            pltpu.VMEM((2 * PER, 8, 16, 8, 128), f32),
            pltpu.VMEM((8, 2 * PER, 8, 128), f32),
            pltpu.VMEM((2 * PER, 8, 8, 128), f32),
            pltpu.SemaphoreType.DMA((8,)),
            pltpu.SemaphoreType.DMA((4, 2, GROUPS)),
            pltpu.SemaphoreType.DMA((4, 2, GROUPS)),
            pltpu.SemaphoreType.DMA((4, 3)),
            pltpu.SemaphoreType.DMA((4, 3)),
            pltpu.SemaphoreType.DMA((4,)),
        ],
        compiler_params=pltpu.CompilerParams(
            collective_id=0, has_side_effects=True, vmem_limit_bytes=24 << 20
        ),
        cost_estimate=pl.CostEstimate(
            flops=2_000_000_000, bytes_accessed=4_000_000, transcendentals=0
        ),
    )(*(pltpu.with_memory_space_constraint(array, pltpu.HBM) for array in operands))
    return (result[0], result[1], result[2], result[3])


def solution(mesh):
    return jax.shard_map(
        on_device,
        mesh=mesh,
        in_specs=(
            P("lev", "lat", None),
            P("lev", "lat", None),
            P("lev", "lat", None),
            P("lev", "lat", None),
            P(),
        ),
        out_specs=(
            P(None, "lat", "lev"),
            P(None, "lat", "lev"),
            P(None, "lat", "lev"),
            P(None, "lat", "lev"),
        ),
        check_vma=False,
    )
```

```python
import math

import jax
import jax.numpy as jnp
import numpy as np
from jax import lax
from jax.experimental import pallas as pl
from jax.experimental.pallas import tpu as pltpu
from jax.sharding import PartitionSpec as P

SPEED = 0.04
QUARTER = math.cos(math.pi / 4.0)
SPACING = 180.0 / 1440.0
LON = 2880
ROWS = 4
LEVELS = 4
GROUPS = 4
COARSE = 12
FINE = 240
WIDE = 256
EDGE = 8
PER = COARSE // GROUPS
WAVES = COARSE // 2 + 1
ORDER = (2, 3, 1, 0)
MESH = pl.DeviceIdType.MESH


def grid_table(bands):
    f32 = np.float32
    rows = np.arange(bands * ROWS)
    faces = np.arange(bands * ROWS + 1)
    scale = f32(math.pi / 180.0)
    center = np.cos(((rows.astype(f32) + f32(0.5)) * f32(SPACING) - f32(90.0)) * scale)
    face = np.cos((faces.astype(f32) * f32(SPACING) - f32(90.0)) * scale)
    face = np.where(faces == 0, f32(0.0), face)
    table = np.zeros((bands, 4, 8, 128), f32)
    for sub in range(8):
        row = ROWS * np.arange(bands) + sub % ROWS
        table[:, 0, sub] = (f32(1.0) / center[row])[:, None]
        table[:, 1, sub] = face[row + 1][:, None]
        outer = ROWS * np.arange(bands) + (0 if sub % ROWS < 2 else ROWS)
        table[:, 2, sub] = face[outer][:, None]
        table[:, 3, sub] = (center[row] / f32(QUARTER))[:, None]
    return table


def split_bf16(array):
    high = array.astype(jnp.bfloat16)
    low = (array - high.astype(np.float32)).astype(jnp.bfloat16)
    return high, low


def constants():
    cell = np.arange(FINE)
    wave = np.arange(FINE)
    angle = 2.0 * np.pi * (np.outer(cell, wave) % FINE) / FINE
    cos, sin = np.cos(angle), np.sin(angle)
    forward = np.zeros((2 * WIDE, 2 * WIDE))
    spots = slice(EDGE, EDGE + FINE)
    spots_im = slice(WIDE + EDGE, WIDE + EDGE + FINE)
    forward[spots, 0:FINE] = cos
    forward[spots, WIDE : WIDE + FINE] = -sin
    forward[spots_im, 0:FINE] = sin
    forward[spots_im, WIDE : WIDE + FINE] = cos
    backward = np.zeros((2 * WIDE, 2 * WIDE))
    backward[0:FINE, spots] = cos.T
    backward[0:FINE, spots_im] = sin.T
    backward[WIDE : WIDE + FINE, spots] = -sin.T
    backward[WIDE : WIDE + FINE, spots_im] = cos.T
    matrices = np.stack(
        [m for whole in (forward, backward) for m in split_bf16(whole.astype(np.float32))]
    )
    tables = np.zeros((3, 8, WIDE), np.float32)
    for order in range(WAVES):
        turn = 2.0 * np.pi * order * cell / LON
        tables[0, order, spots] = np.cos(turn)
        tables[1, order, spots] = np.sin(turn)
        number = (order + COARSE * wave).astype(np.float32)
        tables[2, order, 0:FINE] = np.sin(number * np.float32(math.pi / LON))
    return matrices, tables


def cos_of(index):
    value = math.cos(2.0 * math.pi * index / COARSE)
    return round(value) if abs(value - round(value)) < 1e-9 else round(2 * value) / 2 if abs(
        2 * value - round(2 * value)
    ) < 1e-9 else value


def combine(terms):
    total = None
    for factor, array in terms:
        if factor == 0:
            continue
        if total is None:
            total = array if factor == 1 else -array if factor == -1 else factor * array
        elif factor == 1:
            total = total + array
        elif factor == -1:
            total = total - array
        else:
            total = total + factor * array
    return total


def forward_blocks(x):
    even = {n: x[n] + x[COARSE - n] for n in range(1, 6)}
    odd = {n: x[n] - x[COARSE - n] for n in range(1, 6)}
    ends = {0: x[0] + x[6], 1: x[0] - x[6]}
    even_sum = {n: even[n] + even[6 - n] for n in (1, 2)}
    even_dif = {n: even[n] - even[6 - n] for n in (1, 2)}
    odd_sum = {n: odd[n] + odd[6 - n] for n in (1, 2)}
    odd_dif = {n: odd[n] - odd[6 - n] for n in (1, 2)}
    real, imag = [], []
    for k in range(WAVES):
        pick = even_dif if k % 2 else even_sum
        terms = [(1, ends[k % 2])] + [(cos_of(n * k), pick[n]) for n in (1, 2)]
        terms.append((cos_of(3 * k), even[3]))
        real.append(combine(terms))
        if 0 < k < 6:
            pick = odd_sum if k % 2 else odd_dif
            terms = [(-cos_of(n * k - 3), pick[n]) for n in (1, 2)]
            terms.append((-cos_of(3 * k - 3), odd[3]))
            imag.append(combine(terms))
        else:
            imag.append(None)
    return real, imag


def backward_blocks(real, imag):
    base = {0: real[0] + real[6], 1: real[0] - real[6]}
    blocks = [None] * COARSE
    for b in range(0, 7):
        cosine = combine([(1, base[b % 2])] + [(cos_of(k * b), real[k]) for k in range(1, 6)])
        if b in (0, 6):
            blocks[b] = cosine
            continue
        sine = combine([(-cos_of(k * b - 3), imag[k]) for k in range(1, 6)])
        blocks[b] = cosine + sine
        blocks[COARSE - b] = cosine - sine
    return blocks


def minmod(left, right):
    return jnp.maximum(jnp.minimum(left, right), 0.0) + jnp.minimum(jnp.maximum(left, right), 0.0)


def window(load, block):
    lane = lax.broadcasted_iota(jnp.int32, (8, WIDE), 1)
    if block == 0:
        body = pltpu.roll(load(0, 256), EDGE, 1)
        tail = pltpu.roll(load(2816, LON), 128 - (LON - EDGE - 2816), 1)
        return jnp.concatenate(
            [jnp.where(lane[:, :128] < EDGE, tail, body[:, :128]), body[:, 128:]], axis=1
        )
    start = FINE * block - EDGE
    first = start // 128 * 128
    body = pltpu.roll(load(first, first + 384), (384 - (start - first)) % 384, 1)[:, :WIDE]
    if block == COARSE - 1:
        head = pltpu.roll(load(0, 256), WIDE - EDGE, 1)
        body = jnp.where(lane >= WIDE - EDGE, head, body)
    return body


def limits(courant):
    return jnp.where(courant >= 0.0, 0.5, -0.5) - 0.5 * courant


def kernel(
    grid_hbm, share_hbm, u_hbm, v_hbm, t_hbm, h_hbm, mat_hbm, tab_hbm,
    out_ref,
    given, mat_ref, tab_ref, grid_ref, share_ref,
    own, to_up, to_down, from_down, from_up, base, lean_ref, inverse_h,
    field, sent, held, spread, gain, z_hi, z_lo, weight, wide, target_ref,
    in_sem, halo_send, halo_recv, turn_send, turn_recv, own_sem,
):
    bands = lax.axis_size("lat")
    band = lax.axis_index("lat")
    group = lax.axis_index("lev")
    above = (lax.rem(band + 1, bands), group)
    below = (lax.rem(band + bands - 1, bands), group)
    partners = [(band, lax.rem(group + step, GROUPS)) for step in range(1, GROUPS)]

    has_below, has_above = band > 0, band < bands - 1
    barrier = pltpu.get_barrier_semaphore()

    def greet(device):
        pl.semaphore_signal(barrier, inc=1, device_id=device, device_id_type=MESH)

    for device in partners:
        greet(device)
    pl.when(has_below)(lambda: greet(below))
    pl.when(has_above)(lambda: greet(above))

    loads = [
        pltpu.make_async_copy(source, given.at[item], in_sem.at[item])
        for item, source in enumerate((h_hbm, v_hbm, u_hbm, t_hbm))
    ]
    tables = [
        pltpu.make_async_copy(grid_hbm.at[band], grid_ref, in_sem.at[4]),
        pltpu.make_async_copy(tab_hbm, tab_ref, in_sem.at[5]),
        pltpu.make_async_copy(share_hbm, share_ref, in_sem.at[6]),
        pltpu.make_async_copy(mat_hbm, mat_ref, in_sem.at[7]),
    ]
    for copy in loads + tables[:3]:
        copy.start()

    @pl.when(jnp.logical_not(has_below))
    def _():
        from_down[...] = jnp.zeros_like(from_down)

    @pl.when(jnp.logical_not(has_above))
    def _():
        from_up[...] = jnp.zeros_like(from_up)

    def sub_row(shape):
        return lax.rem(lax.broadcasted_iota(jnp.int32, shape, 0), ROWS)

    place = sub_row((8, WIDE))

    def down(array, step):
        return pltpu.roll(array, step % 8, 0)

    def side(array, step):
        return pltpu.roll(array, step % WIDE, 1)

    def cut_item(item):
        for pair in range(2):

            def load(first, last):
                value = given[item, 2 * pair : 2 * pair + 2, :, first : min(last, LON)]
                value = value.reshape(8, min(last, LON) - first)
                short = -value.shape[1] % 128
                if short:
                    value = jnp.concatenate([value, jnp.zeros((8, short), jnp.float32)], axis=1)
                return value

            for block in range(COARSE):
                own[item, block, pair] = window(load, block)

        def edges(block, carry):
            a, b = own[item, block, 0], own[item, block, 1]
            to_up[item, block] = jnp.where(
                place < 2,
                jnp.where(place == 0, down(a, -3), down(b, -2)),
                jnp.where(place == 2, a, down(b, 1)),
            )
            to_down[item, block] = jnp.where(
                place < 2,
                jnp.where(place == 0, down(b, -1), a),
                jnp.where(place == 2, down(b, 2), down(a, 3)),
            )
            return carry

        lax.fori_loop(0, COARSE, edges, 0)

    def home(step):
        return PER * lax.rem(group + step, GROUPS)

    def halo(item, way, step):
        spot = (item, pl.ds(home(step), PER)) if item < 2 else (item,)
        return pltpu.make_async_remote_copy(
            src_ref=(to_down if way else to_up).at[spot],
            dst_ref=(from_up if way else from_down).at[spot],
            send_sem=halo_send.at[item, way, step],
            recv_sem=halo_recv.at[item, way, step],
            device_id=below if way else above,
            device_id_type=MESH,
        )

    def start_halo(item, step=0):
        pl.when(has_above)(lambda: halo(item, 0, step).start())
        pl.when(has_below)(lambda: halo(item, 1, step).start())

    def drain_halo(item, step=0):
        pl.when(has_above)(lambda: halo(item, 0, step).wait_send())
        pl.when(has_below)(lambda: halo(item, 1, step).wait_send())

    for item in range(4):
        loads[item].wait()
        cut_item(item)
        if item == 0:
            pl.semaphore_wait(
                barrier,
                len(partners) + jnp.where(has_below, 1, 0) + jnp.where(has_above, 1, 0),
            )
        if item == 1:
            tables[3].start()
            for step in ORDER:
                start_halo(0, step)
                start_halo(1, step)
        elif item == 2:
            start_halo(2)
    for copy in tables:
        copy.wait()

    def zonal(block, carry):
        for pair in range(2):
            wind = own[2, block, pair]
            thick = own[0, block, pair]
            c = SPEED * (wind + side(wind, -1))
            up = c >= 0.0
            part = limits(c)
            for item in range(4):
                q = thick if item == 0 else thick * own[item, block, pair]
                before, after, later = side(q, 1), side(q, -1), side(q, -2)
                step = after - q
                first = jnp.where(up, q - before, later - after)
                through = c * (jnp.where(up, q, after) + part * minmod(first, step))
                base[item, block, pair] = q - (through - side(through, 1))
        return carry

    lax.fori_loop(0, COARSE, zonal, 0, unroll=2)

    start_halo(3)
    ratio = jnp.concatenate([grid_ref[3], grid_ref[3]], axis=1)
    for order in range(WAVES):
        sine = jnp.broadcast_to(tab_ref[2, order : order + 1, :], (8, WIDE))
        damping = ratio / jnp.maximum(sine, ratio)
        damping = damping * damping * ((1.0 if order in (0, 6) else 2.0) / LON)
        gain[16 * order : 16 * order + 8] = damping
        gain[16 * order + 8 : 16 * order + 16] = damping


    def outer(a, b):
        return jnp.where(
            place == 1, down(b, 1), jnp.where(place == 2, down(b, -1), a)
        )

    def wide_grid(index):
        return jnp.concatenate([grid_ref[index], grid_ref[index]], axis=1)

    def slants(block, carry):
        a, b = own[1, block, 0], own[1, block, 1]
        near = jnp.where(place < 2, from_down[1, block], from_up[1, block])
        winds = (a + down(a, -1), b + down(b, -1), near + outer(a, b))
        for index, wind in enumerate(winds):
            c = SPEED * wind
            lean_ref[block, 2 * index] = c * wide_grid(2 if index == 2 else 1)
            lean_ref[block, 2 * index + 1] = limits(c)
        return carry

    def meridional(item, step=None):
        def one(block, carry):
            if step is not None:
                block = home(step) + block
                slants(block, carry)
            sign = jnp.where(place < 2, 1.0, -1.0)
            low, high = from_down[0, block], from_up[0, block]
            cells = [own[0, block, 0], own[0, block, 1]]
            if item:
                low, high = low * from_down[item, block], high * from_up[item, block]
                cells = [cells[pair] * own[item, block, pair] for pair in range(2)]
            near = jnp.where(place < 2, low, high)
            far = jnp.where(place < 2, down(low, -2), down(high, 2))
            edge = outer(*cells)
            gap = edge - near
            near_slope = sign * minmod(near - far, gap)
            gap = sign * gap
            slopes, flows = [], []
            for pair in range(2):
                x = cells[pair]
                after = down(x, -1)
                inner = after - x
                upper = jnp.where(place == 3, down(gap, 1) if pair else gap, inner)
                lower = jnp.where(place == 0, down(gap, -1) if pair else gap, down(inner, 1))
                slope = minmod(lower, upper)
                slopes.append(slope)
                part = lean_ref[block, 2 * pair + 1]
                up = part > 0.0
                flows.append(
                    lean_ref[block, 2 * pair]
                    * (jnp.where(up, x, after) + part * jnp.where(up, slope, down(slope, -1)))
                )
            part = lean_ref[block, 5]
            pick = part * sign > 0.0
            flow = lean_ref[block, 4] * (
                jnp.where(pick, near, edge) + part * jnp.where(pick, near_slope, outer(*slopes))
            )
            for pair in range(2):
                above_flow = jnp.where(place == 3, down(flow, 1) if pair else flow, flows[pair])
                below_flow = jnp.where(
                    place == 0, down(flow, -1) if pair else flow, down(flows[pair], 1)
                )
                value = base[item, block, pair] - (above_flow - below_flow) * wide_grid(0)
                rows = pl.ds(8 * pair, 8)
                if item == 0:
                    sent[0, block, rows] = value
                    inverse_h[block, rows] = 1.0 / value
                else:
                    field[block, rows] = value * inverse_h[block, rows]
            return carry

        if step is None:
            lax.fori_loop(0, COARSE, one, 0, unroll=2)
        else:
            lax.fori_loop(0, PER, one, 0, unroll=True)

    def turn(item, step):
        target = lax.rem(group + step, GROUPS)
        return pltpu.make_async_remote_copy(
            src_ref=sent.at[item, pl.ds(PER * target, PER)],
            dst_ref=held.at[item, group],
            send_sem=turn_send.at[item, step - 1],
            recv_sem=turn_recv.at[item, step - 1],
            device_id=(band, target),
            device_id_type=MESH,
        )

    def keep(item):
        return pltpu.make_async_copy(
            sent.at[item, pl.ds(PER * group, PER)], held.at[item, group], own_sem.at[item]
        )

    def start_turn(item):
        for step in (2, 3, 1):
            turn(item, step).start()
        keep(item).start()

    def end_turn(item):
        for step in range(1, GROUPS):
            source = lax.rem(group + GROUPS - step, GROUPS)
            pltpu.make_async_remote_copy(
                src_ref=sent.at[item, pl.ds(0, PER)],
                dst_ref=held.at[item, source],
                send_sem=turn_send.at[item, step - 1],
                recv_sem=turn_recv.at[item, step - 1],
                device_id=(band, source),
                device_id_type=MESH,
            ).wait_recv()
        keep(item).wait()

    def product(index):
        high, low = z_hi[...], z_lo[...]
        return (
            jnp.dot(high, mat_ref[index], preferred_element_type=jnp.float32)
            + jnp.dot(low, mat_ref[index], preferred_element_type=jnp.float32)
            + jnp.dot(high, mat_ref[index + 1], preferred_element_type=jnp.float32)
        )

    def polar(item):
        def forward(tile, carry):
            lanes = pl.ds(pl.multiple_of(128 * tile, 128), 128)
            real, imag = forward_blocks([field[block, :, lanes] for block in range(COARSE)])
            for order in range(WAVES):
                cos = jnp.broadcast_to(tab_ref[0, order : order + 1, lanes], (16, 128))
                sin = jnp.broadcast_to(tab_ref[1, order : order + 1, lanes], (16, 128))
                if imag[order] is None:
                    parts = (real[order] * cos, -(real[order] * sin))
                else:
                    parts = (
                        real[order] * cos + imag[order] * sin,
                        imag[order] * cos - real[order] * sin,
                    )
                for half, part in enumerate(parts):
                    at = pl.multiple_of(WIDE * half + 128 * tile, 128)
                    spot = (pl.ds(16 * order, 16), pl.ds(at, 128))
                    high = part.astype(jnp.bfloat16)
                    z_hi[spot] = high
                    z_lo[spot] = (part - high.astype(jnp.float32)).astype(jnp.bfloat16)
            return carry

        lax.fori_loop(0, 2, forward, 0, unroll=True)
        damping = gain[...]
        waves = product(0) * jnp.concatenate([damping, damping], axis=1)
        high = waves.astype(jnp.bfloat16)
        z_hi[...] = high
        z_lo[...] = (waves - high.astype(jnp.float32)).astype(jnp.bfloat16)
        spread[...] = product(2)

        def backward(tile, carry):
            lanes = pl.ds(pl.multiple_of(128 * tile, 128), 128)
            other = pl.ds(pl.multiple_of(WIDE + 128 * tile, 128), 128)
            real, imag = [], []
            for order in range(WAVES):
                rows = pl.ds(16 * order, 16)
                cos = jnp.broadcast_to(tab_ref[0, order : order + 1, lanes], (16, 128))
                sin = jnp.broadcast_to(tab_ref[1, order : order + 1, lanes], (16, 128))
                re, im = spread[rows, lanes], spread[rows, other]
                real.append(re * cos - im * sin)
                imag.append(im * cos + re * sin)
            for block, value in enumerate(backward_blocks(real, imag)):
                sent[item, block, :, lanes] = value
            return carry

        lax.fori_loop(0, 2, backward, 0, unroll=True)

    def end_halo(item, step=0):
        pl.when(has_below)(lambda: halo(item, 0, step).wait_recv())
        pl.when(has_above)(lambda: halo(item, 1, step).wait_recv())

    for step in ORDER:
        end_halo(0, step)
        end_halo(1, step)
        meridional(0, step)
        if step:
            turn(0, step).start()
        else:
            keep(0).start()
    for item in range(1, 4):
        if item > 1:
            end_halo(item)
        meridional(item)
        polar(item)
        start_turn(item)
    for step in ORDER:
        drain_halo(0, step)
        drain_halo(1, step)
    drain_halo(2)
    drain_halo(3)

    first_half = lax.broadcasted_iota(jnp.int32, (8, 128), 0) < ROWS

    def lines(item, block, lanes):
        found = []
        for index in range(8):
            both = held[item, index // 2, block, pl.ds(8 * (index % 2), 8), lanes]
            turned = down(both, ROWS)
            found.append(jnp.where(first_half, both, turned))
            found.append(jnp.where(first_half, turned, both))
        return found

    def tile_of(step):
        return step // 2, pl.ds(pl.multiple_of(128 * lax.rem(step, 2), 128), 128)

    def weigh(step, carry):
        uppers = []
        for line in lines(0, *tile_of(step)):
            uppers.append(uppers[-1] + line if uppers else line)
        total = uppers[-1]
        lowers = [jnp.zeros((8, 128), jnp.float32)] + uppers[:-1]
        running = share_ref[0]
        for level in range(1, 16):
            running = running + share_ref[level]
        unit = total / jnp.full((8, 128), running)
        running = jnp.float32(0.0)
        for pair in range(8):
            one, two = share_ref[2 * pair], share_ref[2 * pair + 1]
            target = unit * jnp.where(first_half, one, two)
            top = unit * jnp.where(first_half, running + one, running + one + two)
            running = running + one + two
            bottom = top - target
            wide[pair, step] = target
            target_ref[step, pair] = 1.0 / target
            for index in range(16):
                weight[step, pair, index] = jnp.maximum(
                    jnp.minimum(top, uppers[index]) - jnp.maximum(bottom, lowers[index]), 0.0
                )
        return carry

    def gather(item):
        def one(step, carry):
            found = lines(item, *tile_of(step))
            for pair in range(8):
                total = weight[step, pair, 0] * found[0]
                for index in range(1, 16):
                    total = total + weight[step, pair, index] * found[index]
                wide[pair, step] = total * target_ref[step, pair]
            return carry

        lax.fori_loop(0, 2 * PER, one, 0, unroll=2)

    def pack(output):
        def one(pair, carry):
            lane = lax.broadcasted_iota(jnp.int32, (8, 128), 1)
            shifts = (128 - EDGE, 104, 88)
            t = [pltpu.roll(wide[pair, step], shifts[step // 2], 1) for step in range(6)]
            tiles = [
                jnp.where(lane < 120, t[0], t[1]),
                jnp.where(lane < 112, t[1], t[2]),
                jnp.where(lane < 104, t[2], t[3]),
                jnp.where(lane < 96, t[3], t[4]),
                jnp.where(lane < 88, t[4], t[5]),
                t[5],
            ]
            for at, tile in enumerate(tiles):
                size = min(128, LON // GROUPS - 128 * at)
                value = tile[:, :size].reshape(2, ROWS, size)
                out_ref[output, pl.ds(2 * pair, 2), :, 128 * at : 128 * at + size] = value
            return carry

        lax.fori_loop(0, 8, one, 0, unroll=True)

    end_turn(0)
    lax.fori_loop(0, 2 * PER, weigh, 0)
    pack(3)
    for item in range(1, 4):
        end_turn(item)
        gather(item)
        pack((0, 2, 1, 0)[item])

    for item in range(4):
        for step in range(1, GROUPS):
            turn(item, step).wait_send()


def on_device(
    zonal_velocity, meridional_velocity, heat_anomaly, layer_pressure_depth, reference_layer_shares
):
    matrices, tables = constants()
    f32 = jnp.float32
    hbm = pl.BlockSpec(memory_space=pltpu.HBM)
    size = 16 * WAVES
    operands = (
        jnp.asarray(grid_table(lax.axis_size("lat"))),
        reference_layer_shares,
        zonal_velocity,
        meridional_velocity,
        heat_anomaly,
        layer_pressure_depth,
        jnp.asarray(matrices),
        jnp.asarray(tables),
    )
    result = pl.pallas_call(
        kernel,
        out_shape=jax.ShapeDtypeStruct((4, 16, ROWS, LON // GROUPS), f32),
        in_specs=[hbm] * 8,
        out_specs=pl.BlockSpec(memory_space=pltpu.VMEM),
        scratch_shapes=[
            pltpu.VMEM((4, LEVELS, ROWS, LON), f32),
            pltpu.VMEM((4, 2 * WIDE, 2 * WIDE), jnp.bfloat16),
            pltpu.VMEM((3, 8, WIDE), f32),
            pltpu.VMEM((4, 8, 128), f32),
            pltpu.SMEM((16,), f32),
            pltpu.VMEM((4, COARSE, 2, 8, WIDE), f32),
            pltpu.VMEM((4, COARSE, 8, WIDE), f32),
            pltpu.VMEM((4, COARSE, 8, WIDE), f32),
            pltpu.VMEM((4, COARSE, 8, WIDE), f32),
            pltpu.VMEM((4, COARSE, 8, WIDE), f32),
            pltpu.VMEM((4, COARSE, 2, 8, WIDE), f32),
            pltpu.VMEM((COARSE, 6, 8, WIDE), f32),
            pltpu.VMEM((COARSE, 16, WIDE), f32),
            pltpu.VMEM((COARSE, 16, WIDE), f32),
            pltpu.VMEM((4, COARSE, 16, WIDE), f32),
            pltpu.VMEM((4, GROUPS, PER, 16, WIDE), f32),
            pltpu.VMEM((size, 2 * WIDE), f32),
            pltpu.VMEM((size, WIDE), f32),
            pltpu.VMEM((size, 2 * WIDE), jnp.bfloat16),
            pltpu.VMEM((size, 2 * WIDE), jnp.bfloat16),
            pltpu.VMEM((2 * PER, 8, 16, 8, 128), f32),
            pltpu.VMEM((8, 2 * PER, 8, 128), f32),
            pltpu.VMEM((2 * PER, 8, 8, 128), f32),
            pltpu.SemaphoreType.DMA((8,)),
            pltpu.SemaphoreType.DMA((4, 2, GROUPS)),
            pltpu.SemaphoreType.DMA((4, 2, GROUPS)),
            pltpu.SemaphoreType.DMA((4, 3)),
            pltpu.SemaphoreType.DMA((4, 3)),
            pltpu.SemaphoreType.DMA((4,)),
        ],
        compiler_params=pltpu.CompilerParams(
            collective_id=0, has_side_effects=True, vmem_limit_bytes=24 << 20
        ),
        cost_estimate=pl.CostEstimate(
            flops=2_000_000_000, bytes_accessed=4_000_000, transcendentals=0
        ),
    )(*(pltpu.with_memory_space_constraint(array, pltpu.HBM) for array in operands))
    return (result[0], result[1], result[2], result[3])


def solution(mesh):
    return jax.shard_map(
        on_device,
        mesh=mesh,
        in_specs=(
            P("lev", "lat", None),
            P("lev", "lat", None),
            P("lev", "lat", None),
            P("lev", "lat", None),
            P(),
        ),
        out_specs=(
            P(None, "lat", "lev"),
            P(None, "lat", "lev"),
            P(None, "lat", "lev"),
            P(None, "lat", "lev"),
        ),
        check_vma=False,
    )
```

```python
import math

import jax
import jax.numpy as jnp
import numpy as np
from jax import lax
from jax.experimental import pallas as pl
from jax.experimental.pallas import tpu as pltpu
from jax.sharding import PartitionSpec as P

SPEED = 0.04
QUARTER = math.cos(math.pi / 4.0)
SPACING = 180.0 / 1440.0
LON = 2880
ROWS = 4
LEVELS = 4
GROUPS = 4
COARSE = 12
FINE = 240
WIDE = 256
EDGE = 8
PER = COARSE // GROUPS
WAVES = COARSE // 2 + 1
ORDER = (2, 3, 1, 0)
MESH = pl.DeviceIdType.MESH


def grid_table(bands):
    f32 = np.float32
    rows = np.arange(bands * ROWS)
    faces = np.arange(bands * ROWS + 1)
    scale = f32(math.pi / 180.0)
    center = np.cos(((rows.astype(f32) + f32(0.5)) * f32(SPACING) - f32(90.0)) * scale)
    face = np.cos((faces.astype(f32) * f32(SPACING) - f32(90.0)) * scale)
    face = np.where(faces == 0, f32(0.0), face)
    table = np.zeros((bands, 4, 8, 128), f32)
    for sub in range(8):
        row = ROWS * np.arange(bands) + sub % ROWS
        table[:, 0, sub] = (f32(1.0) / center[row])[:, None]
        table[:, 1, sub] = face[row + 1][:, None]
        outer = ROWS * np.arange(bands) + (0 if sub % ROWS < 2 else ROWS)
        table[:, 2, sub] = face[outer][:, None]
        table[:, 3, sub] = (center[row] / f32(QUARTER))[:, None]
    return table


def split_bf16(array):
    high = array.astype(jnp.bfloat16)
    low = (array - high.astype(np.float32)).astype(jnp.bfloat16)
    return high, low


def constants():
    cell = np.arange(FINE)
    wave = np.arange(FINE)
    angle = 2.0 * np.pi * (np.outer(cell, wave) % FINE) / FINE
    cos, sin = np.cos(angle), np.sin(angle)
    forward = np.zeros((2 * WIDE, 2 * WIDE))
    spots = slice(EDGE, EDGE + FINE)
    spots_im = slice(WIDE + EDGE, WIDE + EDGE + FINE)
    forward[spots, 0:FINE] = cos
    forward[spots, WIDE : WIDE + FINE] = -sin
    forward[spots_im, 0:FINE] = sin
    forward[spots_im, WIDE : WIDE + FINE] = cos
    backward = np.zeros((2 * WIDE, 2 * WIDE))
    backward[0:FINE, spots] = cos.T
    backward[0:FINE, spots_im] = sin.T
    backward[WIDE : WIDE + FINE, spots] = -sin.T
    backward[WIDE : WIDE + FINE, spots_im] = cos.T
    matrices = np.stack(
        [m for whole in (forward, backward) for m in split_bf16(whole.astype(np.float32))]
    )
    tables = np.zeros((3, 8, WIDE), np.float32)
    for order in range(WAVES):
        turn = 2.0 * np.pi * order * cell / LON
        tables[0, order, spots] = np.cos(turn)
        tables[1, order, spots] = np.sin(turn)
        number = (order + COARSE * wave).astype(np.float32)
        tables[2, order, 0:FINE] = np.sin(number * np.float32(math.pi / LON))
    return matrices, tables


def cos_of(index):
    value = math.cos(2.0 * math.pi * index / COARSE)
    return round(value) if abs(value - round(value)) < 1e-9 else round(2 * value) / 2 if abs(
        2 * value - round(2 * value)
    ) < 1e-9 else value


def combine(terms):
    total = None
    for factor, array in terms:
        if factor == 0:
            continue
        if total is None:
            total = array if factor == 1 else -array if factor == -1 else factor * array
        elif factor == 1:
            total = total + array
        elif factor == -1:
            total = total - array
        else:
            total = total + factor * array
    return total


def forward_blocks(x):
    even = {n: x[n] + x[COARSE - n] for n in range(1, 6)}
    odd = {n: x[n] - x[COARSE - n] for n in range(1, 6)}
    ends = {0: x[0] + x[6], 1: x[0] - x[6]}
    even_sum = {n: even[n] + even[6 - n] for n in (1, 2)}
    even_dif = {n: even[n] - even[6 - n] for n in (1, 2)}
    odd_sum = {n: odd[n] + odd[6 - n] for n in (1, 2)}
    odd_dif = {n: odd[n] - odd[6 - n] for n in (1, 2)}
    real, imag = [], []
    for k in range(WAVES):
        pick = even_dif if k % 2 else even_sum
        terms = [(1, ends[k % 2])] + [(cos_of(n * k), pick[n]) for n in (1, 2)]
        terms.append((cos_of(3 * k), even[3]))
        real.append(combine(terms))
        if 0 < k < 6:
            pick = odd_sum if k % 2 else odd_dif
            terms = [(-cos_of(n * k - 3), pick[n]) for n in (1, 2)]
            terms.append((-cos_of(3 * k - 3), odd[3]))
            imag.append(combine(terms))
        else:
            imag.append(None)
    return real, imag


def backward_blocks(real, imag):
    base = {0: real[0] + real[6], 1: real[0] - real[6]}
    blocks = [None] * COARSE
    for b in range(0, 7):
        cosine = combine([(1, base[b % 2])] + [(cos_of(k * b), real[k]) for k in range(1, 6)])
        if b in (0, 6):
            blocks[b] = cosine
            continue
        sine = combine([(-cos_of(k * b - 3), imag[k]) for k in range(1, 6)])
        blocks[b] = cosine + sine
        blocks[COARSE - b] = cosine - sine
    return blocks


def minmod(left, right):
    return jnp.maximum(jnp.minimum(left, right), 0.0) + jnp.minimum(jnp.maximum(left, right), 0.0)


def window(load, block):
    lane = lax.broadcasted_iota(jnp.int32, (8, WIDE), 1)
    if block == 0:
        body = pltpu.roll(load(0, 256), EDGE, 1)
        tail = pltpu.roll(load(2816, LON), 128 - (LON - EDGE - 2816), 1)
        return jnp.concatenate(
            [jnp.where(lane[:, :128] < EDGE, tail, body[:, :128]), body[:, 128:]], axis=1
        )
    start = FINE * block - EDGE
    first = start // 128 * 128
    body = pltpu.roll(load(first, first + 384), (384 - (start - first)) % 384, 1)[:, :WIDE]
    if block == COARSE - 1:
        head = pltpu.roll(load(0, 256), WIDE - EDGE, 1)
        body = jnp.where(lane >= WIDE - EDGE, head, body)
    return body


def limits(courant):
    return jnp.where(courant >= 0.0, 0.5, -0.5) - 0.5 * courant


def kernel(
    grid_hbm, share_hbm, u_hbm, v_hbm, t_hbm, h_hbm, mat_hbm, tab_hbm,
    out_ref,
    given, mat_ref, tab_ref, grid_ref, share_ref,
    own, to_up, to_down, from_down, from_up, base, lean_ref, inverse_h,
    field, sent, held, spread, gain, z_hi, z_lo, weight, wide, target_ref,
    in_sem, halo_send, halo_recv, turn_send, turn_recv, own_sem,
):
    bands = lax.axis_size("lat")
    band = lax.axis_index("lat")
    group = lax.axis_index("lev")
    above = (lax.rem(band + 1, bands), group)
    below = (lax.rem(band + bands - 1, bands), group)
    beside = group + 1 - 2 * lax.rem(group, 2)
    groups = (group, beside, lax.rem(group + 2, GROUPS), lax.rem(beside + 2, GROUPS))
    partners = [(band, groups[step]) for step in range(1, GROUPS)]

    has_below, has_above = band > 0, band < bands - 1
    barrier = pltpu.get_barrier_semaphore()

    def greet(device):
        pl.semaphore_signal(barrier, inc=1, device_id=device, device_id_type=MESH)

    for device in partners:
        greet(device)
    pl.when(has_below)(lambda: greet(below))
    pl.when(has_above)(lambda: greet(above))

    loads = [
        pltpu.make_async_copy(source, given.at[item], in_sem.at[item])
        for item, source in enumerate((h_hbm, v_hbm, u_hbm, t_hbm))
    ]
    tables = [
        pltpu.make_async_copy(grid_hbm.at[band], grid_ref, in_sem.at[4]),
        pltpu.make_async_copy(tab_hbm, tab_ref, in_sem.at[5]),
        pltpu.make_async_copy(share_hbm, share_ref, in_sem.at[6]),
        pltpu.make_async_copy(mat_hbm, mat_ref, in_sem.at[7]),
    ]
    for copy in loads + tables:
        copy.start()

    @pl.when(jnp.logical_not(has_below))
    def _():
        from_down[...] = jnp.zeros_like(from_down)

    @pl.when(jnp.logical_not(has_above))
    def _():
        from_up[...] = jnp.zeros_like(from_up)

    def sub_row(shape):
        return lax.rem(lax.broadcasted_iota(jnp.int32, shape, 0), ROWS)

    place = sub_row((8, WIDE))

    def down(array, step):
        return pltpu.roll(array, step % 8, 0)

    def side(array, step):
        return pltpu.roll(array, step % WIDE, 1)

    def cut_item(item):
        for pair in range(2):

            def load(first, last):
                value = given[item, 2 * pair : 2 * pair + 2, :, first : min(last, LON)]
                value = value.reshape(8, min(last, LON) - first)
                short = -value.shape[1] % 128
                if short:
                    value = jnp.concatenate([value, jnp.zeros((8, short), jnp.float32)], axis=1)
                return value

            for block in range(COARSE):
                own[item, block, pair] = window(load, block)

        def edges(block, carry):
            a, b = own[item, block, 0], own[item, block, 1]
            to_up[item, block] = jnp.where(
                place < 2,
                jnp.where(place == 0, down(a, -3), down(b, -2)),
                jnp.where(place == 2, a, down(b, 1)),
            )
            to_down[item, block] = jnp.where(
                place < 2,
                jnp.where(place == 0, down(b, -1), a),
                jnp.where(place == 2, down(b, 2), down(a, 3)),
            )
            return carry

        lax.fori_loop(0, COARSE, edges, 0)

    def home(step):
        return PER * groups[step]

    def halo(item, way, step):
        spot = (item, pl.ds(home(step), PER)) if item < 2 else (item,)
        return pltpu.make_async_remote_copy(
            src_ref=(to_down if way else to_up).at[spot],
            dst_ref=(from_up if way else from_down).at[spot],
            send_sem=halo_send.at[item, way, step],
            recv_sem=halo_recv.at[item, way, step],
            device_id=below if way else above,
            device_id_type=MESH,
        )

    def start_halo(item, step=0):
        pl.when(has_above)(lambda: halo(item, 0, step).start())
        pl.when(has_below)(lambda: halo(item, 1, step).start())

    def drain_halo(item, step=0):
        pl.when(has_above)(lambda: halo(item, 0, step).wait_send())
        pl.when(has_below)(lambda: halo(item, 1, step).wait_send())

    for item in range(4):
        loads[item].wait()
        cut_item(item)
        if item == 0:
            pl.semaphore_wait(
                barrier,
                len(partners) + jnp.where(has_below, 1, 0) + jnp.where(has_above, 1, 0),
            )
        if item == 1:
            for step in ORDER:
                start_halo(0, step)
                start_halo(1, step)
        elif item == 2:
            start_halo(2)
    for copy in tables:
        copy.wait()

    def zonal(block, carry):
        for pair in range(2):
            wind = own[2, block, pair]
            thick = own[0, block, pair]
            c = SPEED * (wind + side(wind, -1))
            up = c >= 0.0
            part = limits(c)
            for item in range(4):
                q = thick if item == 0 else thick * own[item, block, pair]
                before, after, later = side(q, 1), side(q, -1), side(q, -2)
                step = after - q
                first = jnp.where(up, q - before, later - after)
                through = c * (jnp.where(up, q, after) + part * minmod(first, step))
                base[item, block, pair] = q - (through - side(through, 1))
        return carry

    lax.fori_loop(0, COARSE, zonal, 0, unroll=2)

    start_halo(3)
    ratio = jnp.concatenate([grid_ref[3], grid_ref[3]], axis=1)
    for order in range(WAVES):
        sine = jnp.broadcast_to(tab_ref[2, order : order + 1, :], (8, WIDE))
        damping = ratio / jnp.maximum(sine, ratio)
        damping = damping * damping * ((1.0 if order in (0, 6) else 2.0) / LON)
        gain[16 * order : 16 * order + 8] = damping
        gain[16 * order + 8 : 16 * order + 16] = damping


    def outer(a, b):
        return jnp.where(
            place == 1, down(b, 1), jnp.where(place == 2, down(b, -1), a)
        )

    def wide_grid(index):
        return jnp.concatenate([grid_ref[index], grid_ref[index]], axis=1)

    def slants(block, carry):
        a, b = own[1, block, 0], own[1, block, 1]
        near = jnp.where(place < 2, from_down[1, block], from_up[1, block])
        winds = (a + down(a, -1), b + down(b, -1), near + outer(a, b))
        for index, wind in enumerate(winds):
            c = SPEED * wind
            lean_ref[block, 2 * index] = c * wide_grid(2 if index == 2 else 1)
            lean_ref[block, 2 * index + 1] = limits(c)
        return carry

    def meridional(item, step=None):
        def one(block, carry):
            if step is not None:
                block = home(step) + block
                slants(block, carry)
            sign = jnp.where(place < 2, 1.0, -1.0)
            low, high = from_down[0, block], from_up[0, block]
            cells = [own[0, block, 0], own[0, block, 1]]
            if item:
                low, high = low * from_down[item, block], high * from_up[item, block]
                cells = [cells[pair] * own[item, block, pair] for pair in range(2)]
            near = jnp.where(place < 2, low, high)
            far = jnp.where(place < 2, down(low, -2), down(high, 2))
            edge = outer(*cells)
            gap = edge - near
            near_slope = sign * minmod(near - far, gap)
            gap = sign * gap
            slopes, flows = [], []
            for pair in range(2):
                x = cells[pair]
                after = down(x, -1)
                inner = after - x
                upper = jnp.where(place == 3, down(gap, 1) if pair else gap, inner)
                lower = jnp.where(place == 0, down(gap, -1) if pair else gap, down(inner, 1))
                slope = minmod(lower, upper)
                slopes.append(slope)
                part = lean_ref[block, 2 * pair + 1]
                up = part > 0.0
                flows.append(
                    lean_ref[block, 2 * pair]
                    * (jnp.where(up, x, after) + part * jnp.where(up, slope, down(slope, -1)))
                )
            part = lean_ref[block, 5]
            pick = part * sign > 0.0
            flow = lean_ref[block, 4] * (
                jnp.where(pick, near, edge) + part * jnp.where(pick, near_slope, outer(*slopes))
            )
            for pair in range(2):
                above_flow = jnp.where(place == 3, down(flow, 1) if pair else flow, flows[pair])
                below_flow = jnp.where(
                    place == 0, down(flow, -1) if pair else flow, down(flows[pair], 1)
                )
                value = base[item, block, pair] - (above_flow - below_flow) * wide_grid(0)
                rows = pl.ds(8 * pair, 8)
                if item == 0:
                    sent[0, block, rows] = value
                    inverse_h[block, rows] = 1.0 / value
                else:
                    field[block, rows] = value * inverse_h[block, rows]
            return carry

        if step is None:
            lax.fori_loop(0, COARSE, one, 0, unroll=2)
        else:
            lax.fori_loop(0, PER, one, 0, unroll=True)

    def turn(item, step):
        target = groups[step]
        return pltpu.make_async_remote_copy(
            src_ref=sent.at[item, pl.ds(PER * target, PER)],
            dst_ref=held.at[item, group],
            send_sem=turn_send.at[item, step - 1],
            recv_sem=turn_recv.at[item, step - 1],
            device_id=(band, target),
            device_id_type=MESH,
        )

    def keep(item):
        return pltpu.make_async_copy(
            sent.at[item, pl.ds(PER * group, PER)], held.at[item, group], own_sem.at[item]
        )

    def start_turn(item):
        for step in (2, 3, 1):
            turn(item, step).start()
        keep(item).start()

    def end_turn(item):
        for step in range(1, GROUPS):
            source = groups[step]
            pltpu.make_async_remote_copy(
                src_ref=sent.at[item, pl.ds(0, PER)],
                dst_ref=held.at[item, source],
                send_sem=turn_send.at[item, step - 1],
                recv_sem=turn_recv.at[item, step - 1],
                device_id=(band, source),
                device_id_type=MESH,
            ).wait_recv()
        keep(item).wait()

    def product(index):
        high, low = z_hi[...], z_lo[...]
        return (
            jnp.dot(high, mat_ref[index], preferred_element_type=jnp.float32)
            + jnp.dot(low, mat_ref[index], preferred_element_type=jnp.float32)
            + jnp.dot(high, mat_ref[index + 1], preferred_element_type=jnp.float32)
        )

    def polar(item):
        def forward(tile, carry):
            lanes = pl.ds(pl.multiple_of(128 * tile, 128), 128)
            real, imag = forward_blocks([field[block, :, lanes] for block in range(COARSE)])
            for order in range(WAVES):
                cos = jnp.broadcast_to(tab_ref[0, order : order + 1, lanes], (16, 128))
                sin = jnp.broadcast_to(tab_ref[1, order : order + 1, lanes], (16, 128))
                if imag[order] is None:
                    parts = (real[order] * cos, -(real[order] * sin))
                else:
                    parts = (
                        real[order] * cos + imag[order] * sin,
                        imag[order] * cos - real[order] * sin,
                    )
                for half, part in enumerate(parts):
                    at = pl.multiple_of(WIDE * half + 128 * tile, 128)
                    spot = (pl.ds(16 * order, 16), pl.ds(at, 128))
                    high = part.astype(jnp.bfloat16)
                    z_hi[spot] = high
                    z_lo[spot] = (part - high.astype(jnp.float32)).astype(jnp.bfloat16)
            return carry

        lax.fori_loop(0, 2, forward, 0, unroll=True)
        damping = gain[...]
        waves = product(0) * jnp.concatenate([damping, damping], axis=1)
        high = waves.astype(jnp.bfloat16)
        z_hi[...] = high
        z_lo[...] = (waves - high.astype(jnp.float32)).astype(jnp.bfloat16)
        spread[...] = product(2)

        def backward(tile, carry):
            lanes = pl.ds(pl.multiple_of(128 * tile, 128), 128)
            other = pl.ds(pl.multiple_of(WIDE + 128 * tile, 128), 128)
            real, imag = [], []
            for order in range(WAVES):
                rows = pl.ds(16 * order, 16)
                cos = jnp.broadcast_to(tab_ref[0, order : order + 1, lanes], (16, 128))
                sin = jnp.broadcast_to(tab_ref[1, order : order + 1, lanes], (16, 128))
                re, im = spread[rows, lanes], spread[rows, other]
                real.append(re * cos - im * sin)
                imag.append(im * cos + re * sin)
            for block, value in enumerate(backward_blocks(real, imag)):
                sent[item, block, :, lanes] = value
            return carry

        lax.fori_loop(0, 2, backward, 0, unroll=True)

    def end_halo(item, step=0):
        pl.when(has_below)(lambda: halo(item, 0, step).wait_recv())
        pl.when(has_above)(lambda: halo(item, 1, step).wait_recv())

    for step in ORDER:
        end_halo(0, step)
        end_halo(1, step)
        meridional(0, step)
        if step:
            turn(0, step).start()
        else:
            keep(0).start()
    for item in range(1, 4):
        if item > 1:
            end_halo(item)
        meridional(item)
        polar(item)
        start_turn(item)
    for step in ORDER:
        drain_halo(0, step)
        drain_halo(1, step)
    drain_halo(2)
    drain_halo(3)

    first_half = lax.broadcasted_iota(jnp.int32, (8, 128), 0) < ROWS

    def lines(item, block, lanes):
        found = []
        for index in range(8):
            both = held[item, index // 2, block, pl.ds(8 * (index % 2), 8), lanes]
            turned = down(both, ROWS)
            found.append(jnp.where(first_half, both, turned))
            found.append(jnp.where(first_half, turned, both))
        return found

    def tile_of(step):
        return step // 2, pl.ds(pl.multiple_of(128 * lax.rem(step, 2), 128), 128)

    def weigh(step, carry):
        uppers = []
        for line in lines(0, *tile_of(step)):
            uppers.append(uppers[-1] + line if uppers else line)
        total = uppers[-1]
        lowers = [jnp.zeros((8, 128), jnp.float32)] + uppers[:-1]
        running = share_ref[0]
        for level in range(1, 16):
            running = running + share_ref[level]
        unit = total / jnp.full((8, 128), running)
        running = jnp.float32(0.0)
        for pair in range(8):
            one, two = share_ref[2 * pair], share_ref[2 * pair + 1]
            target = unit * jnp.where(first_half, one, two)
            top = unit * jnp.where(first_half, running + one, running + one + two)
            running = running + one + two
            bottom = top - target
            wide[pair, step] = target
            target_ref[step, pair] = 1.0 / target
            for index in range(16):
                weight[step, pair, index] = jnp.maximum(
                    jnp.minimum(top, uppers[index]) - jnp.maximum(bottom, lowers[index]), 0.0
                )
        return carry

    def gather(item):
        def one(step, carry):
            found = lines(item, *tile_of(step))
            for pair in range(8):
                total = weight[step, pair, 0] * found[0]
                for index in range(1, 16):
                    total = total + weight[step, pair, index] * found[index]
                wide[pair, step] = total * target_ref[step, pair]
            return carry

        lax.fori_loop(0, 2 * PER, one, 0, unroll=2)

    def pack(output):
        def one(pair, carry):
            lane = lax.broadcasted_iota(jnp.int32, (8, 128), 1)
            shifts = (128 - EDGE, 104, 88)
            t = [pltpu.roll(wide[pair, step], shifts[step // 2], 1) for step in range(6)]
            tiles = [
                jnp.where(lane < 120, t[0], t[1]),
                jnp.where(lane < 112, t[1], t[2]),
                jnp.where(lane < 104, t[2], t[3]),
                jnp.where(lane < 96, t[3], t[4]),
                jnp.where(lane < 88, t[4], t[5]),
                t[5],
            ]
            for at, tile in enumerate(tiles):
                size = min(128, LON // GROUPS - 128 * at)
                value = tile[:, :size].reshape(2, ROWS, size)
                out_ref[output, pl.ds(2 * pair, 2), :, 128 * at : 128 * at + size] = value
            return carry

        lax.fori_loop(0, 8, one, 0, unroll=True)

    end_turn(0)
    lax.fori_loop(0, 2 * PER, weigh, 0)
    pack(3)
    for item in range(1, 4):
        end_turn(item)
        gather(item)
        pack((0, 2, 1, 0)[item])

    for item in range(4):
        for step in range(1, GROUPS):
            turn(item, step).wait_send()


def on_device(
    zonal_velocity, meridional_velocity, heat_anomaly, layer_pressure_depth, reference_layer_shares
):
    matrices, tables = constants()
    f32 = jnp.float32
    hbm = pl.BlockSpec(memory_space=pltpu.HBM)
    size = 16 * WAVES
    operands = (
        jnp.asarray(grid_table(lax.axis_size("lat"))),
        reference_layer_shares,
        zonal_velocity,
        meridional_velocity,
        heat_anomaly,
        layer_pressure_depth,
        jnp.asarray(matrices),
        jnp.asarray(tables),
    )
    result = pl.pallas_call(
        kernel,
        out_shape=jax.ShapeDtypeStruct((4, 16, ROWS, LON // GROUPS), f32),
        in_specs=[hbm] * 8,
        out_specs=pl.BlockSpec(memory_space=pltpu.VMEM),
        scratch_shapes=[
            pltpu.VMEM((4, LEVELS, ROWS, LON), f32),
            pltpu.VMEM((4, 2 * WIDE, 2 * WIDE), jnp.bfloat16),
            pltpu.VMEM((3, 8, WIDE), f32),
            pltpu.VMEM((4, 8, 128), f32),
            pltpu.SMEM((16,), f32),
            pltpu.VMEM((4, COARSE, 2, 8, WIDE), f32),
            pltpu.VMEM((4, COARSE, 8, WIDE), f32),
            pltpu.VMEM((4, COARSE, 8, WIDE), f32),
            pltpu.VMEM((4, COARSE, 8, WIDE), f32),
            pltpu.VMEM((4, COARSE, 8, WIDE), f32),
            pltpu.VMEM((4, COARSE, 2, 8, WIDE), f32),
            pltpu.VMEM((COARSE, 6, 8, WIDE), f32),
            pltpu.VMEM((COARSE, 16, WIDE), f32),
            pltpu.VMEM((COARSE, 16, WIDE), f32),
            pltpu.VMEM((4, COARSE, 16, WIDE), f32),
            pltpu.VMEM((4, GROUPS, PER, 16, WIDE), f32),
            pltpu.VMEM((size, 2 * WIDE), f32),
            pltpu.VMEM((size, WIDE), f32),
            pltpu.VMEM((size, 2 * WIDE), jnp.bfloat16),
            pltpu.VMEM((size, 2 * WIDE), jnp.bfloat16),
            pltpu.VMEM((2 * PER, 8, 16, 8, 128), f32),
            pltpu.VMEM((8, 2 * PER, 8, 128), f32),
            pltpu.VMEM((2 * PER, 8, 8, 128), f32),
            pltpu.SemaphoreType.DMA((8,)),
            pltpu.SemaphoreType.DMA((4, 2, GROUPS)),
            pltpu.SemaphoreType.DMA((4, 2, GROUPS)),
            pltpu.SemaphoreType.DMA((4, 3)),
            pltpu.SemaphoreType.DMA((4, 3)),
            pltpu.SemaphoreType.DMA((4,)),
        ],
        compiler_params=pltpu.CompilerParams(
            collective_id=0, has_side_effects=True, vmem_limit_bytes=24 << 20
        ),
        cost_estimate=pl.CostEstimate(
            flops=2_000_000_000, bytes_accessed=4_000_000, transcendentals=0
        ),
    )(*(pltpu.with_memory_space_constraint(array, pltpu.HBM) for array in operands))
    return (result[0], result[1], result[2], result[3])


def solution(mesh):
    return jax.shard_map(
        on_device,
        mesh=mesh,
        in_specs=(
            P("lev", "lat", None),
            P("lev", "lat", None),
            P("lev", "lat", None),
            P("lev", "lat", None),
            P(),
        ),
        out_specs=(
            P(None, "lat", "lev"),
            P(None, "lat", "lev"),
            P(None, "lat", "lev"),
            P(None, "lat", "lev"),
        ),
        check_vma=False,
    )
```
